128 devices in a mesh: lat: 8 (over x, z_hi), lon: 16 (over y, z_lo, core).
Axes of the slice: x: 4, y: 4, z: 4 (z_hi: 2, z_lo: 2; z = z_hi * 2 + z_lo), core: 2. Of those that a mesh axis runs over, the one named last changes fastest.
Arguments:
- tokens: bfloat16 [32, 4, 352, 512], P('lat', None, 'lon'), may hold values from -6 to 6
- cotangent: bfloat16 [32, 4, 352, 512], P('lat', None, 'lon'), may hold values from -6 to 6
- inproj_lon: bfloat16 [512, 1536], replicated, may hold values from -3 to 3
- outproj_lon: bfloat16 [512, 512], replicated, may hold values from -0.25 to 0.25
- inproj_lat: bfloat16 [512, 1536], replicated, may hold values from -3 to 3
- outproj_lat: bfloat16 [512, 512], replicated, may hold values from -0.25 to 0.25
- mlp_in: bfloat16 [512, 2048], replicated, may hold values from -0.25 to 0.25
- mlp_out: bfloat16 [2048, 512], replicated, may hold values from -0.125 to 0.125
Outputs:
- output: float32 [32, 4, 352, 512], P('lat', None, 'lon')
- grad_tokens: float32 [32, 4, 352, 512], P('lat', None, 'lon')
- grad_inproj_lon: float32 [512, 1536], P(None, ('lat', 'lon'))
- grad_outproj_lon: float32 [512, 512], P(None, ('lat', 'lon'))
- grad_inproj_lat: float32 [512, 1536], P(None, ('lat', 'lon'))
- grad_outproj_lat: float32 [512, 512], P(None, ('lat', 'lon'))
- grad_mlp_in: float32 [512, 2048], P(None, ('lat', 'lon'))
- grad_mlp_out: float32 [2048, 512], P(None, ('lat', 'lon'))
The draws below stay inside these ranges and needn't reach their ends.
All inputs are finite; a program needn't handle non-finite values.
Results may differ from the reference program's by a relative error of at most 0.035.
Values may be sent and summed in bfloat16 or wider, within the bound.
No kernel may reach another device: no remote copies, remote signals or barrier semaphores. Data moves between devices by JAX's collectives and lax.ppermute only.
A program may use at most 128 MiB of HBM per device.

```python
import jax
import jax.numpy as jnp
from jax import lax

D = 512
FF = 2048
HEADS = 8
HEAD_DIM = 64
BATCH = 4
NLAT = 32
NLON = 352


def attention_weights(seed_key):
    subkeys = jax.random.split(seed_key, 6)

    def one_matrix(number):
        normal_part = jnp.clip(jax.random.normal(subkeys[number], (D, D), jnp.float32), -6.0, 6.0)
        return normal_part * D ** (-0.5)
    query_w = one_matrix(0)
    key_w = one_matrix(1)
    value_w = one_matrix(2)
    column = jnp.arange(D)[None, :]
    first_half = column < HEADS // 2 * HEAD_DIM
    query_w = jnp.where(first_half, query_w, query_w)
    key_w = jnp.where(first_half, key_w, key_w)
    return jnp.concatenate([query_w, key_w, value_w], axis=1).astype(jnp.bfloat16)


def draw_inproj_lon(key, part):
    key = jax.random.fold_in(key, 7)
    return attention_weights(key)


def draw_inproj_lat(key, part):
    key = jax.random.fold_in(key, 8)
    return attention_weights(key)


def with_spikes(values, own_key, source, target, shards_of, factor):
    def block_of(position):
        return (jnp.arange(values.shape[position]) // (values.shape[position] // shards_of)).reshape((-1,) + (1,) * (values.ndim - 1 - position))

    one_side = jax.random.permutation(own_key, shards_of)[block_of(target)]
    other_side = (block_of(target) + shards_of // 2) % shards_of
    return jnp.where((block_of(source) == one_side) | (block_of(source) == other_side), factor * values, values)


def levels(rng, extent, cuts, smallest, top_value):
    gain, own = 1.0, jax.random.fold_in(rng, 6)
    for position, blocks in cuts:
        heights = jnp.exp(jax.random.uniform(jax.random.fold_in(own, position), (blocks,), jnp.float32, smallest / len(cuts), top_value / len(cuts)))
        gain = gain * jnp.repeat(heights, extent[position] // blocks).reshape([-1 if axis == position else 1 for axis in range(len(extent))])
    return gain


def bell_draw(own_key, shape, width, reach, cuts=(), kind=jnp.bfloat16):
    values = width * jax.random.normal(own_key, shape, jnp.float32)
    if cuts:
        values = values * levels(own_key, shape, cuts, -0.22, 0.18)
    return jnp.clip(values, -reach, reach).astype(kind)


def heavy_noise(stream_key, shape, deviation, limit, cuts, heavy, held_as=jnp.bfloat16):
    drawn = deviation * jax.random.normal(stream_key, shape, jnp.float32)
    if cuts:
        drawn = drawn * levels(stream_key, shape, cuts, -0.22, 0.18)
    return jnp.clip(with_spikes(drawn, jax.random.fold_in(stream_key, 3), *heavy), -limit, limit).astype(held_as)


def setup_inputs(seed: int = 0) -> dict:
    streams_of = jax.random.split(jax.random.key(seed), 9)
    tokens = bell_draw(streams_of[0], (NLAT, BATCH, NLON, D), 1.0, 6.0, ((0, 8), (2, 16)))
    cotangent = heavy_noise(streams_of[1], (NLAT, BATCH, NLON, D), 1.0, 6.0, ((0, 8), (2, 16)), (0, 3, 8, 2.0))
    inproj_lon = draw_inproj_lon(jax.random.fold_in(streams_of[8], 71), 0)
    outproj_lon = bell_draw(streams_of[3], (D, D), D ** -0.5, 0.25)
    inproj_lat = draw_inproj_lat(jax.random.fold_in(streams_of[8], 71), 0)
    outproj_lat = bell_draw(streams_of[5], (D, D), D ** -0.5, 0.25)
    mlp_in = bell_draw(streams_of[6], (D, FF), D ** -0.5, 0.25)
    mlp_out = bell_draw(streams_of[7], (FF, D), FF ** -0.5, 0.125)
    return dict(tokens=tokens, cotangent=cotangent, inproj_lon=inproj_lon, outproj_lon=outproj_lon, inproj_lat=inproj_lat, outproj_lat=outproj_lat, mlp_in=mlp_in, mlp_out=mlp_out)


EPSILON = 1e-05

def layer_norm(hidden):
    values = hidden.astype(jnp.float32)
    center = values - lax.optimization_barrier(jnp.mean(values, axis=-1, keepdims=True))
    spread = lax.optimization_barrier(jnp.mean(center * center, axis=-1, keepdims=True))
    return (center * lax.rsqrt(spread + EPSILON)).astype(jnp.bfloat16)

def norm_back(hidden, upstream):
    values = hidden.astype(jnp.float32)
    center = values - lax.optimization_barrier(jnp.mean(values, axis=-1, keepdims=True))
    inverse = lax.rsqrt(lax.optimization_barrier(jnp.mean(center * center, axis=-1, keepdims=True)) + EPSILON)
    scaled = center * inverse
    return inverse * (upstream - lax.optimization_barrier(jnp.mean(upstream, axis=-1, keepdims=True)) - scaled * lax.optimization_barrier(jnp.mean(upstream * scaled, axis=-1, keepdims=True)))

def exact_gelu(values):
    return jax.nn.gelu(values, approximate=False)

def project(array, matrix):
    flat = array.reshape(-1, array.shape[-1])
    result = jnp.dot(flat, matrix, preferred_element_type=jnp.float32)
    return result.reshape(array.shape[:-1] + (matrix.shape[1],))

def outer_sum(left, right):
    return jnp.dot(left.reshape(-1, left.shape[-1]).T, right.reshape(-1, right.shape[-1]), preferred_element_type=jnp.float32)

def split_heads(packed, segment):
    length = packed.shape[0]
    sliced = packed[:, segment * D:(segment + 1) * D].astype(jnp.float32)
    return sliced.reshape(length, HEADS, HEAD_DIM)

def head_scores(packed):
    queries = split_heads(packed, 0)
    keys_all = split_heads(packed, 1)
    scores = jnp.einsum('qhe,khe->hqk', queries, keys_all) * HEAD_DIM ** (-0.5)
    return (queries, keys_all, split_heads(packed, 2), scores)

def attend_one(packed):
    queries, keys_all, values_all, scores = head_scores(packed)
    weights = lax.optimization_barrier(jax.nn.softmax(scores, axis=-1).astype(jnp.bfloat16))
    mixed = jnp.einsum('hqk,khe->qhe', weights.astype(jnp.float32), values_all)
    return mixed.reshape(packed.shape[0], D).astype(jnp.bfloat16)

def attend_back_one(packed, upstream):
    length = packed.shape[0]
    queries, keys_all, values_all, scores = head_scores(packed)
    probs = jax.nn.softmax(scores, axis=-1)
    weights = lax.optimization_barrier(probs.astype(jnp.bfloat16)).astype(jnp.float32)
    grad_mix = upstream.astype(jnp.float32).reshape(length, HEADS, HEAD_DIM)
    grad_values = jnp.einsum('hqk,qhe->khe', weights, grad_mix).astype(jnp.bfloat16)
    grad_probs = jnp.einsum('qhe,khe->hqk', grad_mix, values_all)
    grad_scores = probs * (grad_probs - lax.optimization_barrier(jnp.sum(grad_probs * probs, axis=-1, keepdims=True))) * HEAD_DIM ** (-0.5)
    grad_rounded = lax.optimization_barrier(grad_scores.astype(jnp.bfloat16)).astype(jnp.float32)
    grad_queries = jnp.einsum('hqk,khe->qhe', grad_rounded, keys_all).astype(jnp.bfloat16)
    grad_keys = jnp.einsum('hqk,qhe->khe', grad_rounded, queries).astype(jnp.bfloat16)
    return jnp.concatenate([grad_queries.reshape(length, D), grad_keys.reshape(length, D), grad_values.reshape(length, D)], axis=1)

def attend_back_pair(pair_items):
    return attend_back_one(pair_items[0], pair_items[1])

def to_sequences(packed, along_lon):
    columns = packed.shape[-1]
    if along_lon:
        return packed.reshape(NLAT * BATCH, NLON, columns)
    return jnp.transpose(packed.reshape(NLAT, BATCH * NLON, columns), (1, 0, 2))

def from_sequences(sequences, along_lon):
    columns = sequences.shape[-1]
    if along_lon:
        return sequences.reshape(NLAT, BATCH, NLON, columns)
    return jnp.transpose(sequences, (1, 0, 2)).reshape(NLAT, BATCH, NLON, columns)

def forward_sub(hidden, inproj, outproj, along_lon):
    normed = layer_norm(hidden)
    packed = project(normed, inproj).astype(jnp.bfloat16)
    mixed = from_sequences(lax.map(attend_one, to_sequences(packed, along_lon)), along_lon)
    result = hidden.astype(jnp.float32) + project(mixed, outproj)
    return (result, normed, packed, mixed)

def backward_sub(hidden, upstream, normed, packed, mixed, inproj, outproj, along_lon):
    upstream_low = upstream.astype(jnp.bfloat16)
    grad_outproj = outer_sum(mixed, upstream_low)
    grad_mixed = project(upstream_low, outproj.T).astype(jnp.bfloat16)
    grad_packed = from_sequences(lax.map(attend_back_pair, (to_sequences(packed, along_lon), to_sequences(grad_mixed, along_lon))), along_lon)
    grad_inproj = outer_sum(normed, grad_packed)
    grad_normed = project(grad_packed, inproj.T)
    previous = upstream.astype(jnp.float32) + norm_back(hidden, grad_normed)
    return (previous, grad_inproj, grad_outproj)

def reference(tokens, cotangent, inproj_lon, outproj_lon, inproj_lat, outproj_lat, mlp_in, mlp_out):
    hidden_one, normed_one, packed_one, mixed_one = forward_sub(tokens, inproj_lon, outproj_lon, True)
    hidden_two, normed_two, packed_two, mixed_two = forward_sub(hidden_one, inproj_lat, outproj_lat, False)

    def mlp_block(carry, pieces):
        hidden_rows, upstream_rows = pieces
        normed = layer_norm(hidden_rows)
        inner = project(normed, mlp_in)
        activated, pullback = jax.vjp(exact_gelu, inner)
        activated_low = activated.astype(jnp.bfloat16)
        result = hidden_rows.astype(jnp.float32) + project(activated_low, mlp_out)
        grad_act = project(upstream_rows, mlp_out.T)
        grad_inner = pullback(grad_act)[0].astype(jnp.bfloat16)
        grad_normed = project(grad_inner, mlp_in.T)
        previous = upstream_rows.astype(jnp.float32) + norm_back(hidden_rows, grad_normed)
        sums_in = carry[0] + outer_sum(normed, grad_inner)
        sums_out = carry[1] + outer_sum(activated_low, upstream_rows)
        return ((sums_in, sums_out), (result, previous))
    start = (jnp.zeros((D, FF), jnp.float32), jnp.zeros((FF, D), jnp.float32))
    (grad_mlp_in, grad_mlp_out), (output, grad_two) = lax.scan(mlp_block, start, (hidden_two, cotangent))
    grad_one, grad_inproj_lat, grad_outproj_lat = backward_sub(hidden_one, grad_two, normed_two, packed_two, mixed_two, inproj_lat, outproj_lat, False)
    grad_tokens, grad_inproj_lon, grad_outproj_lon = backward_sub(tokens, grad_one, normed_one, packed_one, mixed_one, inproj_lon, outproj_lon, True)
    return (output, grad_tokens, grad_inproj_lon, grad_outproj_lon, grad_inproj_lat, grad_outproj_lat, grad_mlp_in, grad_mlp_out)
```

```python
import jax
import jax.numpy as jnp
from jax import lax
from jax.sharding import Mesh, PartitionSpec as P

HEADS = 8
WIDTH = 512
EPSILON = 1e-05
LON = ("y", "l", "c")
TURN = ("y", "x", "h")
CHIPS = ("x", "h", "y", "l")
f32 = jnp.float32
bf16 = jnp.bfloat16


def normalize(values):
    center = values - jnp.mean(values, axis=-1, keepdims=True)
    inverse = lax.rsqrt(jnp.mean(center * center, axis=-1, keepdims=True) + EPSILON)
    return center * inverse, inverse


def norm_back(scaled, inverse, upstream):
    return inverse * (
        upstream
        - jnp.mean(upstream, axis=-1, keepdims=True)
        - scaled * jnp.mean(upstream * scaled, axis=-1, keepdims=True)
    )


def dot(left, right, dims=((1,), (0,))):
    return lax.dot_general(left, right, (dims, ((), ())), preferred_element_type=f32)


def heads_of(packed, part):
    columns = packed[..., part * WIDTH : (part + 1) * WIDTH]
    return columns.reshape(columns.shape[:-1] + (HEADS, WIDTH // HEADS))


def probabilities(packed):
    scores = jnp.einsum(
        "sqhe,skhe->shqk", heads_of(packed, 0), heads_of(packed, 1), preferred_element_type=f32
    )
    return jax.nn.softmax(scores * (WIDTH // HEADS) ** -0.5, axis=-1)


def attend(packed):
    weights = probabilities(packed).astype(bf16)
    mixed = jnp.einsum("shqk,skhe->sqhe", weights, heads_of(packed, 2), preferred_element_type=f32)
    return mixed.astype(bf16).reshape(packed.shape[:2] + (WIDTH,))


def attend_back(packed, upstream):
    probs = probabilities(packed)
    grad_mix = upstream.reshape(upstream.shape[:2] + (HEADS, WIDTH // HEADS))
    grad_values = jnp.einsum(
        "shqk,sqhe->skhe", probs.astype(bf16), grad_mix, preferred_element_type=f32
    )
    grad_probs = jnp.einsum("sqhe,skhe->shqk", grad_mix, heads_of(packed, 2), preferred_element_type=f32)
    inner = jnp.sum(grad_probs * probs, axis=-1, keepdims=True)
    grad_scores = (probs * (grad_probs - inner) * (WIDTH // HEADS) ** -0.5).astype(bf16)
    grad_queries = jnp.einsum("shqk,skhe->sqhe", grad_scores, heads_of(packed, 1), preferred_element_type=f32)
    grad_keys = jnp.einsum("shqk,sqhe->skhe", grad_scores, heads_of(packed, 0), preferred_element_type=f32)
    parts = [p.astype(bf16).reshape(upstream.shape) for p in (grad_queries, grad_keys, grad_values)]
    return jnp.concatenate(parts, axis=-1)


def forward_sub(hidden, inproj, outproj, shape):
    scaled, _ = normalize(hidden)
    normed = scaled.astype(bf16)
    packed = dot(normed, inproj).astype(bf16)
    mixed = attend(packed.reshape(shape + (3 * WIDTH,))).reshape(-1, WIDTH)
    return hidden + dot(mixed, outproj), (normed, packed, mixed)


def backward_sub(hidden, upstream, saved, inproj, outproj, shape):
    normed, packed, mixed = saved
    low = upstream.astype(bf16)
    grad_outproj = dot(low, mixed, ((0,), (0,)))
    grad_mixed = dot(low, outproj, ((1,), (1,))).astype(bf16)
    grad_packed = attend_back(
        packed.reshape(shape + (3 * WIDTH,)), grad_mixed.reshape(shape + (WIDTH,))
    ).reshape(-1, 3 * WIDTH)
    grad_inproj = dot(grad_packed, normed, ((0,), (0,)))
    grad_normed = dot(grad_packed, inproj, ((1,), (1,)))
    scaled, inverse = normalize(hidden)
    previous = upstream + norm_back(scaled, inverse, grad_normed)
    both = jnp.concatenate([grad_inproj.reshape(128, 12, WIDTH), grad_outproj.reshape(128, 4, WIDTH)], axis=1)
    return previous, both.astype(bf16)


def feed_forward(hidden, cotangent, mlp_in, mlp_out):
    scaled, inverse = normalize(hidden)
    normed = scaled.astype(bf16)
    inner = dot(normed, mlp_in)
    spread = 0.5 * (1.0 + lax.erf(inner * 2.0**-0.5))
    activated = (inner * spread).astype(bf16)
    output = hidden + dot(activated, mlp_out)
    slope = spread + inner * (0.5 / jnp.pi) ** 0.5 * jnp.exp(-0.5 * inner * inner)
    grad_inner = (dot(cotangent, mlp_out, ((1,), (1,))) * slope).astype(bf16)
    grad_normed = dot(grad_inner, mlp_in, ((1,), (1,)))
    grad_two = cotangent.astype(f32) + norm_back(scaled, inverse, grad_normed)
    grad_in = dot(grad_inner, normed, ((0,), (0,)))
    grad_out = dot(cotangent, activated, ((0,), (0,)))
    both = jnp.concatenate([grad_in.reshape(128, 16, WIDTH), grad_out.reshape(128, 16, WIDTH)], axis=1)
    return output, grad_two, both.astype(bf16)


def scatter_sum(terms):
    rows = terms.shape[1]
    pairs = terms.reshape(64, 2, rows, WIDTH)
    core = lax.axis_index("c")
    mine = lax.dynamic_index_in_dim(pairs, core, 1, keepdims=False)
    other = lax.dynamic_index_in_dim(pairs, 1 - core, 1, keepdims=False)
    other = lax.ppermute(other, "c", [(0, 1), (1, 0)])
    both = (mine.astype(f32) + other.astype(f32)).astype(bf16)
    parts = lax.all_to_all(both, CHIPS, split_axis=0, concat_axis=0, tiled=True)
    return jnp.sum(parts.astype(f32), axis=0)


def swap(array, axes):
    return lax.all_to_all(array, axes, split_axis=0, concat_axis=0, tiled=True)


def per_device(tokens, cotangent, inproj_lon, outproj_lon, inproj_lat, outproj_lat, mlp_in, mlp_out):
    pack = jnp.concatenate([tokens, cotangent], axis=2).reshape(16, 44, WIDTH)
    pack = swap(pack, LON)
    row_tokens = pack[:, :22].reshape(352, WIDTH).astype(f32)
    row_cotangent = pack[:, 22:].reshape(32, 11, WIDTH)
    hidden_one, saved_lon = forward_sub(row_tokens, inproj_lon, outproj_lon, (1, 352))
    pack = jnp.concatenate([hidden_one.astype(bf16).reshape(32, 11, WIDTH), row_cotangent], axis=1)
    pack = swap(pack, TURN)
    pack = jnp.transpose(pack, (1, 0, 2)).reshape(2, 352, WIDTH)
    hidden_one = pack[0].astype(f32)
    hidden_two, saved_lat = forward_sub(hidden_one, inproj_lat, outproj_lat, (11, 32))
    output, grad_two, terms_mlp = feed_forward(hidden_two, pack[1], mlp_in, mlp_out)
    grad_one, terms_lat = backward_sub(hidden_one, grad_two, saved_lat, inproj_lat, outproj_lat, (11, 32))
    pack = jnp.concatenate([grad_one.astype(bf16), output.astype(bf16)], axis=0).reshape(22, 32, WIDTH)
    pack = swap(jnp.transpose(pack, (1, 0, 2)), TURN)
    row_grad = pack[:, :11].reshape(352, WIDTH).astype(f32)
    grad_tokens, terms_lon = backward_sub(row_tokens, row_grad, saved_lon, inproj_lon, outproj_lon, (1, 352))
    pack = jnp.concatenate([grad_tokens.astype(bf16).reshape(16, 22, WIDTH), pack[:, 11:].reshape(16, 22, WIDTH)], axis=1)
    pack = swap(pack, LON).reshape(4, 4, 44, WIDTH).astype(f32)
    terms = scatter_sum(jnp.concatenate([terms_lon, terms_lat, terms_mlp], axis=1))
    return (
        pack[:, :, 22:],
        pack[:, :, :22],
        terms[0:12].T,
        terms[12:16].T,
        terms[16:28].T,
        terms[28:32].T,
        terms[32:48].T,
        terms[48:64].reshape(4, 4 * WIDTH).T,
    )


def solution(mesh):
    fine = Mesh(mesh.devices.reshape(4, 2, 4, 2, 2), ("x", "h", "y", "l", "c"))
    grid = P(("x", "h"), None, ("y", "l", "c"), None)
    columns = P(None, ("x", "h", "y", "l", "c"))
    return jax.shard_map(
        per_device,
        mesh=fine,
        in_specs=(grid, grid) + (P(),) * 6,
        out_specs=(grid, grid) + (columns,) * 6,
        check_vma=False,
    )
```

```python
import jax
import jax.numpy as jnp
from jax import lax
from jax.experimental import pallas as pl
from jax.experimental.pallas import tpu as pltpu
from jax.sharding import Mesh, PartitionSpec as P

HEADS = 8
WIDTH = 512
FF = 2048
HEAD = WIDTH // HEADS
SCALE = HEAD**-0.5
EPSILON = 1e-05
ROWS = 352
LATS = 32
NEAR = 22
PART = 11
LON = ("y", "l", "c")
TURN = ("y", "x", "h")
CHIPS = ("x", "h", "y", "l")
WHOLE = ((0, ROWS),)
BLOCKS = ((0, 128), (128, 128), (256, 96))
f32 = jnp.float32
bf16 = jnp.bfloat16


def normalize(values):
    center = values - jnp.mean(values, axis=-1, keepdims=True)
    inverse = lax.rsqrt(jnp.mean(center * center, axis=-1, keepdims=True) + EPSILON)
    return center * inverse, inverse


def norm_back(scaled, inverse, upstream):
    return inverse * (
        upstream
        - jnp.mean(upstream, axis=-1, keepdims=True)
        - scaled * jnp.mean(upstream * scaled, axis=-1, keepdims=True)
    )


def dot(left, right, left_dim=1, right_dim=0):
    dims = (((left_dim,), (right_dim,)), ((), ()))
    return lax.dot_general(left, right, dims, preferred_element_type=f32)


def same_column(rows):
    shape = (rows, rows)
    keys = lax.broadcasted_iota(jnp.int32, shape, 0) // LATS
    return keys == lax.broadcasted_iota(jnp.int32, shape, 1) // LATS


def probabilities(keys, queries, masked):
    scores = dot(keys, queries, 1, 1)
    if masked:
        scores = jnp.where(same_column(scores.shape[0]), scores, -1e30)
    powers = jnp.exp(scores - jnp.max(scores, axis=0, keepdims=True))
    return powers * (1.0 / jnp.sum(powers, axis=0, keepdims=True))


def half_of(values, half):
    lanes = lax.broadcasted_iota(jnp.int32, values.shape, 1) // HEAD
    return jnp.where(lanes == half, values, jnp.zeros_like(values))


def pair_columns(part, pair):
    return pl.ds(pl.multiple_of(part * WIDTH + pair * 2 * HEAD, 2 * HEAD), 2 * HEAD)


def attend(packed, turned, blocks):
    masked = len(blocks) > 1

    def one_pair(pair, _):
        for first, count in blocks:
            rows = pl.ds(first, count)
            queries, keys, values = (packed[rows, pair_columns(p, pair)] for p in range(3))
            for half in range(2):
                probs = probabilities(half_of(keys * SCALE, half), queries, masked).astype(bf16)
                mixed = dot(values, probs, 0, 0)
                place = pl.ds(pl.multiple_of(pair * 2 * HEAD + half * HEAD, HEAD), HEAD)
                turned[place, rows] = mixed[half * HEAD : (half + 1) * HEAD]
        return 0

    lax.fori_loop(0, HEADS // 2, one_pair, 0)


def attend_back(packed, upstream, grads, blocks):
    masked = len(blocks) > 1

    def one_pair(pair, _):
        for first, count in blocks:
            rows = pl.ds(first, count)
            queries, keys, values = (packed[rows, pair_columns(p, pair)] for p in range(3))
            grad_mix = upstream[rows, pair_columns(0, pair)]
            found = []
            for half in range(2):
                probs = probabilities(half_of(keys * SCALE, half), queries, masked)
                grad_probs = dot(half_of(values, half), grad_mix, 1, 1)
                inner = jnp.sum(grad_probs * probs, axis=0, keepdims=True)
                grad_scores = (probs * (grad_probs - inner) * SCALE).astype(bf16)
                found.append(
                    (
                        dot(grad_scores, keys, 0, 0),
                        dot(grad_scores, queries),
                        dot(probs.astype(bf16), grad_mix),
                    )
                )
            for part in range(3):
                joined = half_of(found[0][part], 0) + half_of(found[1][part], 1)
                grads[rows, pair_columns(part, pair)] = joined.astype(bf16)
        return 0

    lax.fori_loop(0, HEADS // 2, one_pair, 0)


def project(normed, inproj, packed):
    for part in range(3):
        columns = pl.ds(part * WIDTH, WIDTH)
        packed[:, columns] = dot(normed, inproj[:, columns]).astype(bf16)


def row_forward(pack, inproj, outproj, out, tokens, normed, packed, mixed, hidden, cotangent, turned):
    for block in range(16):
        piece = pack[block].astype(f32)
        rows = pl.ds(block * NEAR, NEAR)
        hidden[rows, :] = piece[:NEAR]
        cotangent[rows, :] = piece[NEAR:]
    values = hidden[...]
    tokens[...] = values.astype(bf16)
    normed[...] = normalize(values)[0].astype(bf16)
    project(normed[...], inproj, packed)
    attend(packed, turned, WHOLE)
    mixed[...] = turned[...].T.astype(bf16)
    hidden[...] += dot(mixed[...], outproj[...])
    for block in range(LATS):
        rows = pl.ds(block * PART, PART)
        out[block] = jnp.concatenate([hidden[rows, :], cotangent[rows, :]], axis=0).astype(bf16)


def row_backward(pack, tokens, packed, inproj, outproj, out, grads, low, hidden, output, upstream):
    for block in range(LATS):
        piece = pack[block].astype(f32)
        rows = pl.ds(block * PART, PART)
        hidden[rows, :] = piece[:PART]
        output[rows, :] = piece[PART:]
    low[...] = hidden[...].astype(bf16)
    upstream[...] = dot(low[...], outproj[...], 1, 1).astype(bf16)
    attend_back(packed, upstream, grads, WHOLE)
    grad_normed = dot(grads[...], inproj[...], 1, 1)
    hidden[...] += norm_back(*normalize(tokens[...].astype(f32)), grad_normed)
    for block in range(16):
        rows = pl.ds(block * NEAR, NEAR)
        out[block] = jnp.concatenate([hidden[rows, :], output[rows, :]], axis=0).astype(bf16)


def to_columns(pack, first, second):
    for lat in range(LATS):
        piece = pack[lat].astype(f32)
        for tile in range(4):
            lanes = slice(tile * 128, (tile + 1) * 128)
            first[tile, pl.ds(lat, PART, stride=LATS), :] = piece[:PART, lanes]
            second[tile, pl.ds(lat, PART, stride=LATS), :] = piece[PART:, lanes]


def joined(tiles):
    return jnp.concatenate([tiles[tile] for tile in range(4)], axis=1)


def put_tiles(tiles, values):
    for tile in range(4):
        tiles[tile] = values[:, tile * 128 : (tile + 1) * 128]


def from_columns(out, first, second):
    for lat in range(LATS):
        rows = pl.ds(lat, PART, stride=LATS)
        parts = [
            jnp.concatenate([tiles[tile, rows, :] for tile in range(4)], axis=1)
            for tiles in (first, second)
        ]
        out[lat] = jnp.concatenate(parts, axis=0).astype(bf16)


def column_both(
    pack, inproj, outproj, mlp_in, mlp_out,
    out, normed, mixed, grads, low, normed_mlp, activated, grad_inner, cotangent,
    first, second, turned, packed, hidden_one, hidden_two, grad_normed, output, grad_mix,
):
    to_columns(pack, first, second)
    hidden_one[...] = joined(first)
    cotangent[...] = joined(second).astype(bf16)
    normed[...] = normalize(hidden_one[...])[0].astype(bf16)
    project(normed[...], inproj, packed)
    attend(packed, turned, BLOCKS)
    mixed[...] = turned[...].T.astype(bf16)
    hidden_two[...] = hidden_one[...] + dot(mixed[...], outproj[...])
    normed_mlp[...] = normalize(hidden_two[...])[0].astype(bf16)
    output[...] = hidden_two[...]
    grad_normed[...] = jnp.zeros_like(grad_normed)

    def one_chunk(chunk, _):
        columns = pl.ds(pl.multiple_of(chunk * 256, 256), 256)
        inner = dot(normed_mlp[...], mlp_in[:, columns])
        spread = 0.5 * (1.0 + lax.erf(inner * 2.0**-0.5))
        slope = spread + inner * (0.5 / jnp.pi) ** 0.5 * jnp.exp(-0.5 * inner * inner)
        active = (inner * spread).astype(bf16)
        activated[:, columns] = active
        output[...] += dot(active, mlp_out[columns, :])
        grad = (dot(cotangent[...], mlp_out[columns, :], 1, 1) * slope).astype(bf16)
        grad_inner[:, columns] = grad
        grad_normed[...] += dot(grad, mlp_in[:, columns], 1, 1)
        return 0

    lax.fori_loop(0, FF // 256, one_chunk, 0)
    put_tiles(second, output[...])
    grad_two = cotangent[...].astype(f32) + norm_back(*normalize(hidden_two[...]), grad_normed[...])
    hidden_two[...] = grad_two
    low[...] = grad_two.astype(bf16)
    grad_mix[...] = dot(low[...], outproj[...], 1, 1).astype(bf16)
    attend_back(packed, grad_mix, grads, BLOCKS)
    back = norm_back(*normalize(hidden_one[...]), dot(grads[...], inproj[...], 1, 1))
    put_tiles(first, hidden_two[...] + back)
    from_columns(out, first, second)


def part_cores(core, terms, mine, other, block, row):
    pairs = terms.reshape(16, 2, 16, WIDTH)
    blocks, rows = pl.ds(block * 16, 16), pl.ds(row, 16)
    mine[blocks, rows, :] = jnp.where(core == 0, pairs[:, 0], pairs[:, 1]).astype(bf16)
    other[blocks, rows, :] = jnp.where(core == 0, pairs[:, 1], pairs[:, 0]).astype(bf16)


def attention_terms(core, grads, normed, low, mixed, mine, other, row):
    for block in range(4):
        wide = dot(grads[:, block * 384 : (block + 1) * 384], normed[...], 0, 0)
        slim = dot(low[:, block * 128 : (block + 1) * 128], mixed[...], 0, 0)
        terms = [wide.reshape(32, 12, WIDTH), slim.reshape(32, 4, WIDTH)]
        part_cores(core, jnp.concatenate(terms, axis=1), mine, other, block, row)


def row_terms(core, grads, normed, low, mixed, mine, other):
    attention_terms(core[0], grads, normed, low, mixed, mine, other, 0)


def column_terms(
    core, grads, normed, low, mixed, normed_mlp, activated, grad_inner, cotangent, mine, other
):
    attention_terms(core[0], grads, normed, low, mixed, mine, other, 0)
    for block in range(4):
        terms = dot(grad_inner[:, block * 512 : (block + 1) * 512], normed_mlp[...], 0, 0)
        part_cores(core[0], terms.reshape(32, 16, WIDTH), mine, other, block, 16)
        terms = dot(cotangent[:, block * 128 : (block + 1) * 128], activated[...], 0, 0)
        quarters = [
            terms[:, part * WIDTH : (part + 1) * WIDTH].reshape(32, 4, WIDTH) for part in range(4)
        ]
        part_cores(core[0], jnp.concatenate(quarters, axis=1), mine, other, block, 32)


def call(kernel, outs, scratch, args, megabytes, gigaflops, scalars=0):
    return pl.pallas_call(
        kernel,
        out_shape=[jax.ShapeDtypeStruct(shape, kind) for shape, kind in outs],
        in_specs=[pl.BlockSpec(memory_space=pltpu.SMEM)] * scalars
        + [pl.BlockSpec(memory_space=pltpu.VMEM)] * (len(args) - scalars),
        out_specs=[pl.BlockSpec(memory_space=pltpu.VMEM)] * len(outs),
        scratch_shapes=[pltpu.VMEM(shape, kind) for shape, kind in scratch],
        compiler_params=pltpu.CompilerParams(vmem_limit_bytes=megabytes << 20),
        cost_estimate=pl.CostEstimate(
            flops=int(gigaflops * 1e9), bytes_accessed=4 << 20, transcendentals=1 << 20
        ),
    )(*args)


def swap(array, axes):
    return lax.all_to_all(array, axes, split_axis=0, concat_axis=0, tiled=True)


def scatter_sum(mine, other):
    other = lax.ppermute(other, "c", [(0, 1), (1, 0)])
    both = (mine.astype(f32) + other.astype(f32)).astype(bf16)
    return jnp.sum(swap(both, CHIPS).astype(f32), axis=0)


NARROW = (ROWS, WIDTH)
QKV = (ROWS, 3 * WIDTH)
WIDE = (ROWS, FF)
TILES = (4, ROWS, 128)


def per_device(tokens, cotangent, inproj_lon, outproj_lon, inproj_lat, outproj_lat, mlp_in, mlp_out):
    core = lax.axis_index("c").astype(jnp.int32).reshape(1)
    pack = jnp.concatenate([tokens, cotangent], axis=2).reshape(16, 2 * NEAR, WIDTH)
    pack, row_tokens, row_normed, row_packed, row_mixed = call(
        row_forward,
        [((LATS, 2 * PART, WIDTH), bf16), (NARROW, bf16), (NARROW, bf16), (QKV, bf16), (NARROW, bf16)],
        [(NARROW, f32), (NARROW, f32), ((WIDTH, ROWS), f32)],
        (swap(pack, LON), inproj_lon, outproj_lon),
        40,
        1.3,
    )
    pack, *saved = call(
        column_both,
        [((LATS, 2 * PART, WIDTH), bf16), (NARROW, bf16), (NARROW, bf16), (QKV, bf16), (NARROW, bf16)]
        + [(NARROW, bf16), (WIDE, bf16), (WIDE, bf16), (NARROW, bf16)],
        [(TILES, f32), (TILES, f32), ((WIDTH, ROWS), f32), (QKV, bf16)]
        + [(NARROW, f32)] * 4
        + [(NARROW, bf16)],
        (swap(pack, TURN), inproj_lat, outproj_lat, mlp_in, mlp_out),
        48,
        5.0,
    )
    normed, mixed, grads, low, normed_mlp, activated, grad_inner, column_cotangent = saved
    column_mine, column_other = call(
        column_terms,
        [((64, 48, WIDTH), bf16)] * 2,
        [],
        (core, grads, normed, low, mixed, normed_mlp, activated, grad_inner, column_cotangent),
        48,
        2.2,
        scalars=1,
    )
    pack, grads, low = call(
        row_backward,
        [((16, 2 * NEAR, WIDTH), bf16), (QKV, bf16), (NARROW, bf16)],
        [(NARROW, f32), (NARROW, f32), (NARROW, bf16)],
        (swap(pack, TURN), row_tokens, row_packed, inproj_lon, outproj_lon),
        40,
        2.0,
    )
    row_mine, row_other = call(
        row_terms,
        [((64, 16, WIDTH), bf16)] * 2,
        [],
        (core, grads, row_normed, low, row_mixed),
        40,
        0.75,
        scalars=1,
    )
    pack = swap(pack, LON).reshape(4, 4, 2 * NEAR, WIDTH).astype(f32)
    columns = scatter_sum(column_mine, column_other)
    rows = scatter_sum(row_mine, row_other)
    return (
        pack[:, :, NEAR:],
        pack[:, :, :NEAR],
        rows[0:12].T,
        rows[12:16].T,
        columns[0:12].T,
        columns[12:16].T,
        columns[16:32].T,
        columns[32:48].reshape(4, 4, WIDTH).transpose(0, 2, 1).reshape(FF, 4),
    )


def solution(mesh):
    fine = Mesh(mesh.devices.reshape(4, 2, 4, 2, 2), ("x", "h", "y", "l", "c"))
    grid = P(("x", "h"), None, ("y", "l", "c"), None)
    columns = P(None, ("x", "h", "y", "l", "c"))
    return jax.shard_map(
        per_device,
        mesh=fine,
        in_specs=(grid, grid) + (P(),) * 6,
        out_specs=(grid, grid) + (columns,) * 6,
        check_vma=False,
    )
```

```python
import jax
import jax.numpy as jnp
from jax import lax
from jax.experimental import pallas as pl
from jax.experimental.pallas import tpu as pltpu
from jax.sharding import Mesh, PartitionSpec as P

HEADS = 8
WIDTH = 512
FF = 2048
HEAD = WIDTH // HEADS
SCALE = HEAD**-0.5
EPSILON = 1e-05
ROWS = 352
LATS = 32
NEAR = 22
PART = 11
LON = ("y", "l", "c")
TURN = ("y", "x", "h")
CHIPS = ("x", "h", "y", "l")
UNROLL = 1
GRANT = 56
BLOCKS = ((0, 128), (128, 128), (256, 96))
f32 = jnp.float32
bf16 = jnp.bfloat16


def normalize(values):
    center = values - jnp.mean(values, axis=-1, keepdims=True)
    inverse = lax.rsqrt(jnp.mean(center * center, axis=-1, keepdims=True) + EPSILON)
    return center * inverse, inverse


def norm_back(scaled, inverse, upstream):
    return inverse * (
        upstream
        - jnp.mean(upstream, axis=-1, keepdims=True)
        - scaled * jnp.mean(upstream * scaled, axis=-1, keepdims=True)
    )


def dot(left, right, left_dim=1, right_dim=0):
    dims = (((left_dim,), (right_dim,)), ((), ()))
    return lax.dot_general(left, right, dims, preferred_element_type=f32)


def half_of(values, half):
    lanes = lax.broadcasted_iota(jnp.int32, values.shape, 1) // HEAD
    return jnp.where(lanes == half, values, jnp.zeros_like(values))


def pair_columns(part, pair):
    return pl.ds(pl.multiple_of(part * WIDTH + pair * 2 * HEAD, 2 * HEAD), 2 * HEAD)


def over_pairs(body):
    lax.fori_loop(0, HEADS // 2, lambda pair, _: body(pair) or 0, 0, unroll=UNROLL)


def row_probabilities(packed, pair, half):
    keys = half_of(packed[:, pair_columns(1, pair)] * SCALE, half)
    scores = dot(keys, packed[:, pair_columns(0, pair)], 1, 1)
    powers = jnp.exp(scores - jnp.max(scores, axis=0, keepdims=True))
    return (powers * (1.0 / jnp.sum(powers, axis=0, keepdims=True))).astype(bf16)


def put_mixed(turned, pair, half, rows, mixed):
    place = pl.ds(pl.multiple_of(pair * 2 * HEAD + half * HEAD, HEAD), HEAD)
    turned[place, rows] = mixed[half * HEAD : (half + 1) * HEAD]


def put_grads(grads, pair, rows, found):
    for part in range(3):
        both = half_of(found[0][part], 0) + half_of(found[1][part], 1)
        grads[rows, pair_columns(part, pair)] = both.astype(bf16)


def attend_rows(packed, turned):
    def one_pair(pair):
        values = packed[:, pair_columns(2, pair)]
        probs = [row_probabilities(packed, pair, half) for half in range(2)]
        for half in range(2):
            put_mixed(turned, pair, half, pl.ds(0, ROWS), dot(values, probs[half], 0, 0))

    over_pairs(one_pair)


def row_weights(packed_far, weights_far, packed, weights, semaphores):
    mover = Mover(semaphores)
    mover.start(packed_far, packed).wait()

    def one_pair(pair):
        for half in range(2):
            weights[pair * 2 + half] = row_probabilities(packed, pair, half)

    over_pairs(one_pair)
    mover.start(weights, weights_far).wait()


def attend_rows_back(packed, upstream, weights, grads):
    def one_pair(pair):
        queries, keys, values = (packed[:, pair_columns(p, pair)] for p in range(3))
        grad_mix = upstream[:, pair_columns(0, pair)]
        found = []
        for half in range(2):
            low = weights[pair * 2 + half]
            probs = low.astype(f32)
            grad_probs = dot(half_of(values, half), grad_mix, 1, 1)
            inner = jnp.sum(grad_probs * probs, axis=0, keepdims=True)
            grad_scores = (probs * (grad_probs - inner) * SCALE).astype(bf16)
            found.append(
                (dot(grad_scores, keys, 0, 0), dot(grad_scores, queries), dot(low, grad_mix))
            )
        put_grads(grads, pair, pl.ds(0, ROWS), found)

    over_pairs(one_pair)


def column_lanes(count):
    return lax.broadcasted_iota(jnp.int32, (LATS, count), 1) // LATS


def own_columns(square):
    count = square.shape[0]
    lanes = column_lanes(count)
    kept = square[:LATS]
    for column in range(1, count // LATS):
        kept = jnp.where(lanes == column, square[column * LATS : (column + 1) * LATS], kept)
    return kept


def to_square(kept):
    count = kept.shape[1]
    lanes = column_lanes(count)
    parts = [jnp.where(lanes == column, kept, 0.0) for column in range(count // LATS)]
    return jnp.concatenate(parts, axis=0).astype(bf16)


def attend_columns(packed, turned, probs):
    def scores(pair):
        for first, count in BLOCKS:
            rows = pl.ds(first, count)
            queries, keys = (packed[rows, pair_columns(p, pair)] for p in range(2))
            for half in range(2):
                square = dot(half_of(keys * SCALE, half), queries, 1, 1)
                probs[pair * 2 + half, :, rows] = own_columns(square)

    over_pairs(scores)
    powers = probs[...]
    powers = jnp.exp(powers - jnp.max(powers, axis=1, keepdims=True))
    probs[...] = powers * (1.0 / jnp.sum(powers, axis=1, keepdims=True))

    def mix(pair):
        for first, count in BLOCKS:
            rows = pl.ds(first, count)
            values = packed[rows, pair_columns(2, pair)]
            for half in range(2):
                square = to_square(probs[pair * 2 + half, :, rows])
                put_mixed(turned, pair, half, rows, dot(values, square, 0, 0))

    over_pairs(mix)


def attend_columns_back(packed, upstream, probs, grad_scores, grads):
    def products(pair):
        for first, count in BLOCKS:
            rows = pl.ds(first, count)
            values, grad_mix = packed[rows, pair_columns(2, pair)], upstream[rows, pair_columns(0, pair)]
            for half in range(2):
                square = dot(half_of(values, half), grad_mix, 1, 1)
                grad_scores[pair * 2 + half, :, rows] = own_columns(square)

    over_pairs(products)
    grad_probs = grad_scores[...]
    inner = jnp.sum(grad_probs * probs[...], axis=1, keepdims=True)
    grad_scores[...] = probs[...] * (grad_probs - inner) * SCALE

    def combine(pair):
        for first, count in BLOCKS:
            rows = pl.ds(first, count)
            queries, keys = (packed[rows, pair_columns(p, pair)] for p in range(2))
            grad_mix = upstream[rows, pair_columns(0, pair)]
            found = []
            for half in range(2):
                square = to_square(grad_scores[pair * 2 + half, :, rows])
                weights = to_square(probs[pair * 2 + half, :, rows])
                found.append(
                    (dot(square, keys, 0, 0), dot(square, queries), dot(weights, grad_mix))
                )
            put_grads(grads, pair, rows, found)

    over_pairs(combine)


def project(normed, inproj, packed):
    for part in range(3):
        columns = pl.ds(part * WIDTH, WIDTH)
        packed[:, columns] = dot(normed, inproj[:, columns]).astype(bf16)


class Mover:
    def __init__(self, semaphores):
        self.semaphores, self.count = semaphores, 0

    def start(self, source, target):
        copy = pltpu.make_async_copy(source, target, self.semaphores.at[self.count])
        self.count += 1
        copy.start()
        return copy


def row_forward(
    pack, inproj_far, outproj_far,
    out, tokens_far, normed_far, packed_far, mixed_far,
    inproj, outproj, tokens, normed, packed, mixed, hidden, cotangent, turned, semaphores,
):
    mover = Mover(semaphores)
    inproj_in = mover.start(inproj_far, inproj)
    outproj_in = mover.start(outproj_far, outproj)
    for block in range(16):
        piece = pack[block].astype(f32)
        rows = pl.ds(block * NEAR, NEAR)
        hidden[rows, :] = piece[:NEAR]
        cotangent[rows, :] = piece[NEAR:]
    values = hidden[...]
    tokens[...] = values.astype(bf16)
    normed[...] = normalize(values)[0].astype(bf16)
    leaving = [mover.start(tokens, tokens_far), mover.start(normed, normed_far)]
    inproj_in.wait()
    project(normed[...], inproj, packed)
    leaving.append(mover.start(packed, packed_far))
    attend_rows(packed, turned)
    mixed[...] = turned[...].T.astype(bf16)
    leaving.append(mover.start(mixed, mixed_far))
    outproj_in.wait()
    hidden[...] += dot(mixed[...], outproj[...])
    for block in range(LATS):
        rows = pl.ds(block * PART, PART)
        out[block] = jnp.concatenate([hidden[rows, :], cotangent[rows, :]], axis=0).astype(bf16)
    for copy in leaving:
        copy.wait()


def row_backward(
    pack, tokens_far, packed_far, weights_far, inproj_far, outproj_far,
    out, grads_far, low_far,
    tokens, packed, weights, inproj, outproj, grads, low, hidden, output, upstream, semaphores,
):
    mover = Mover(semaphores)
    outproj_in = mover.start(outproj_far, outproj)
    coming = [mover.start(packed_far, packed), mover.start(weights_far, weights)]
    inproj_in = mover.start(inproj_far, inproj)
    tokens_in = mover.start(tokens_far, tokens)
    for block in range(LATS):
        piece = pack[block].astype(f32)
        rows = pl.ds(block * PART, PART)
        hidden[rows, :] = piece[:PART]
        output[rows, :] = piece[PART:]
    low[...] = hidden[...].astype(bf16)
    leaving = [mover.start(low, low_far)]
    outproj_in.wait()
    upstream[...] = dot(low[...], outproj[...], 1, 1).astype(bf16)
    for copy in coming:
        copy.wait()
    attend_rows_back(packed, upstream, weights, grads)
    leaving.append(mover.start(grads, grads_far))
    inproj_in.wait()
    grad_normed = dot(grads[...], inproj[...], 1, 1)
    tokens_in.wait()
    hidden[...] += norm_back(*normalize(tokens[...].astype(f32)), grad_normed)
    for block in range(16):
        rows = pl.ds(block * NEAR, NEAR)
        out[block] = jnp.concatenate([hidden[rows, :], output[rows, :]], axis=0).astype(bf16)
    for copy in leaving:
        copy.wait()


def to_columns(pack, first, second):
    for lat in range(LATS):
        piece = pack[lat].astype(f32)
        for tile in range(4):
            lanes = slice(tile * 128, (tile + 1) * 128)
            first[tile, pl.ds(lat, PART, stride=LATS), :] = piece[:PART, lanes]
            second[tile, pl.ds(lat, PART, stride=LATS), :] = piece[PART:, lanes]


def joined(tiles):
    return jnp.concatenate([tiles[tile] for tile in range(4)], axis=1)


def put_tiles(tiles, values):
    for tile in range(4):
        tiles[tile] = values[:, tile * 128 : (tile + 1) * 128]


def from_columns(out, first, second):
    for lat in range(LATS):
        rows = pl.ds(lat, PART, stride=LATS)
        parts = [
            jnp.concatenate([tiles[tile, rows, :] for tile in range(4)], axis=1)
            for tiles in (first, second)
        ]
        out[lat] = jnp.concatenate(parts, axis=0).astype(bf16)


def column_both(
    pack, inproj_far, outproj_far, mlp_in_far, mlp_out_far,
    out, normed_far, mixed_far, grads_far, low_far, normed_mlp_far, activated_far, grad_inner_far, cotangent_far,
    inproj, outproj, mlp_in, mlp_out, normed, mixed, grads, low, normed_mlp, activated, grad_inner, cotangent,
    packed, upstream, first, second, turned, hidden_one, hidden, grad_normed, output, probs, grad_scores,
    semaphores,
):
    mover = Mover(semaphores)
    inproj_in = mover.start(inproj_far, inproj)
    outproj_in = mover.start(outproj_far, outproj)
    coming = [mover.start(mlp_in_far, mlp_in), mover.start(mlp_out_far, mlp_out)]
    to_columns(pack, first, second)
    hidden_one[...] = joined(first)
    cotangent[...] = joined(second).astype(bf16)
    normed[...] = normalize(hidden_one[...])[0].astype(bf16)
    leaving = [mover.start(cotangent, cotangent_far), mover.start(normed, normed_far)]
    inproj_in.wait()
    project(normed[...], inproj, packed)
    attend_columns(packed, turned, probs)
    mixed[...] = turned[...].T.astype(bf16)
    leaving.append(mover.start(mixed, mixed_far))
    outproj_in.wait()
    hidden[...] = hidden_one[...] + dot(mixed[...], outproj[...])
    normed_mlp[...] = normalize(hidden[...])[0].astype(bf16)
    leaving.append(mover.start(normed_mlp, normed_mlp_far))
    output[...] = hidden[...]
    grad_normed[...] = jnp.zeros_like(grad_normed)
    for copy in coming:
        copy.wait()

    def one_chunk(chunk, _):
        columns = pl.ds(pl.multiple_of(chunk * 512, 512), 512)
        inner = dot(normed_mlp[...], mlp_in[:, columns])
        spread = 0.5 * (1.0 + lax.erf(inner * 2.0**-0.5))
        slope = spread + inner * (0.5 / jnp.pi) ** 0.5 * jnp.exp(-0.5 * inner * inner)
        active = (inner * spread).astype(bf16)
        activated[:, columns] = active
        output[...] += dot(active, mlp_out[columns, :])
        grad = (dot(cotangent[...], mlp_out[columns, :], 1, 1) * slope).astype(bf16)
        grad_inner[:, columns] = grad
        grad_normed[...] += dot(grad, mlp_in[:, columns], 1, 1)
        return 0

    lax.fori_loop(0, FF // 512, one_chunk, 0)
    leaving.append(mover.start(activated, activated_far))
    leaving.append(mover.start(grad_inner, grad_inner_far))
    put_tiles(second, output[...])
    back = norm_back(*normalize(hidden[...]), grad_normed[...])
    hidden[...] = cotangent[...].astype(f32) + back
    low[...] = hidden[...].astype(bf16)
    leaving.append(mover.start(low, low_far))
    upstream[...] = dot(low[...], outproj[...], 1, 1).astype(bf16)
    attend_columns_back(packed, upstream, probs, grad_scores, grads)
    leaving.append(mover.start(grads, grads_far))
    back = norm_back(*normalize(hidden_one[...]), dot(grads[...], inproj[...], 1, 1))
    put_tiles(first, hidden[...] + back)
    from_columns(out, first, second)
    for copy in leaving:
        copy.wait()


def mlp_terms(
    core, normed_far, activated_far, grad_inner_far, cotangent_far, mine_far, other_far,
    normed, activated, grad_inner, cotangent, mine, other, semaphores,
):
    mover = Mover(semaphores)
    soon = [mover.start(grad_inner_far, grad_inner), mover.start(normed_far, normed)]
    coming = [mover.start(cotangent_far, cotangent), mover.start(activated_far, activated)]
    for copy in soon:
        copy.wait()
    leaving = []
    for block in range(4):
        inner = dot(grad_inner[:, block * 512 : (block + 1) * 512], normed[...], 0, 0)
        if block == 0:
            for copy in coming:
                copy.wait()
        outer = dot(cotangent[:, block * 128 : (block + 1) * 128], activated[...], 0, 0)
        quarters = [
            outer[:, part * WIDTH : (part + 1) * WIDTH].reshape(32, 4, WIDTH) for part in range(4)
        ]
        both = jnp.concatenate([inner.reshape(32, 16, WIDTH)] + quarters, axis=1)
        both = both.astype(bf16).reshape(2, 4, 2, 2, 32, WIDTH)
        for high in range(2):
            even, odd = both[high, :, :, 0], both[high, :, :, 1]
            mine[block, high] = jnp.where(core[0] == 0, even, odd)
            other[block, high] = jnp.where(core[0] == 0, odd, even)
            leaving.append(mover.start(mine.at[block, high], mine_far.at[:, block, high]))
            leaving.append(mover.start(other.at[block, high], other_far.at[:, block, high]))
    for copy in leaving:
        copy.wait()


def attention_terms(
    core, grads_far, normed_far, low_far, mixed_far, mine, other, grads, normed, low, mixed, semaphores
):
    mover = Mover(semaphores)
    pairs = ((grads_far, grads), (normed_far, normed), (low_far, low), (mixed_far, mixed))
    for copy in [mover.start(far, near) for far, near in pairs]:
        copy.wait()
    for block in range(4):
        wide = dot(grads[:, block * 384 : (block + 1) * 384], normed[...], 0, 0)
        slim = dot(low[:, block * 128 : (block + 1) * 128], mixed[...], 0, 0)
        terms = [wide.reshape(32, 12, WIDTH), slim.reshape(32, 4, WIDTH)]
        terms = jnp.concatenate(terms, axis=1).astype(bf16).reshape(16, 2, 16, WIDTH)
        chips = pl.ds(block * 16, 16)
        mine[chips] = jnp.where(core[0] == 0, terms[:, 0], terms[:, 1])
        other[chips] = jnp.where(core[0] == 0, terms[:, 1], terms[:, 0])


def join_cores(lon_mine, lon_other, lat_mine, lat_other, out):
    for block in range(4):
        chips = pl.ds(block * 16, 16)
        lon = lon_mine[chips].astype(f32) + lon_other[chips].astype(f32)
        lat = lat_mine[chips].astype(f32) + lat_other[chips].astype(f32)
        out[chips] = jnp.concatenate([lon, lat], axis=1).astype(bf16)


def add_cores(mine_far, other_far, out_far, mine, other, semaphores):
    mover = Mover(semaphores)
    coming = [
        (mover.start(mine_far.at[block], mine.at[block]), mover.start(other_far.at[block], other.at[block]))
        for block in range(4)
    ]
    leaving = []
    for block in range(4):
        for copy in coming[block]:
            copy.wait()
        mine[block] = (mine[block].astype(f32) + other[block].astype(f32)).astype(bf16)
        leaving.append(mover.start(mine.at[block], out_far.at[block]))
    for copy in leaving:
        copy.wait()


def after_both(first, second, out):
    del first, second, out


SMEM, VMEM, HBM = pltpu.SMEM, pltpu.VMEM, pltpu.HBM


def call(kernel, args, outs, scratch, semaphores, gigaflops, aliases=None):
    arrays, places = zip(*args)
    scratch = [pltpu.VMEM(shape, kind) for shape, kind in scratch]
    if semaphores:
        scratch.append(pltpu.SemaphoreType.DMA((semaphores,)))
    return pl.pallas_call(
        kernel,
        out_shape=[jax.ShapeDtypeStruct(shape, kind) for shape, kind, _ in outs],
        in_specs=[pl.BlockSpec(memory_space=place) for place in places],
        out_specs=[pl.BlockSpec(memory_space=place) for _, _, place in outs],
        scratch_shapes=scratch,
        compiler_params=pltpu.CompilerParams(vmem_limit_bytes=GRANT << 20),
        cost_estimate=pl.CostEstimate(
            flops=int(gigaflops * 1e9), bytes_accessed=1 << 16, transcendentals=0
        ),
        input_output_aliases=aliases or {},
    )(*arrays)


def swap(array, axes):
    return lax.all_to_all(array, axes, split_axis=0, concat_axis=0, tiled=True)


def from_other_core(array):
    return lax.ppermute(array, "c", [(0, 1), (1, 0)])


NARROW = (ROWS, WIDTH)
QKV = (ROWS, 3 * WIDTH)
WIDE = (ROWS, FF)
TILES = (4, ROWS, 128)
TURNED = (WIDTH, ROWS)
TO_TURN = (LATS, 2 * PART, WIDTH)
TO_LON = (16, 2 * NEAR, WIDTH)
LON_WEIGHTS = (HEADS, ROWS, ROWS)
LAT_PROBS = (HEADS, LATS, ROWS)
IN, OUT, MLP_IN, MLP_OUT = (WIDTH, 3 * WIDTH), (WIDTH, WIDTH), (WIDTH, FF), (FF, WIDTH)
SUMS = (64, 16, WIDTH)
BY_CHIP, HELD = (4, 4, 2, 2, 32, WIDTH), (4, 2, 4, 2, 32, WIDTH)


def low(*shapes):
    return [(shape, bf16) for shape in shapes]


def far(*shapes):
    return [(shape, bf16, HBM) for shape in shapes]


def all_far(*arrays):
    return [(array, HBM) for array in arrays]


def weight_terms(core, grads, normed, low_upstream, mixed):
    return call(
        attention_terms,
        [(core, SMEM)] + all_far(grads, normed, low_upstream, mixed),
        [(SUMS, bf16, VMEM)] * 2,
        low(QKV, NARROW, NARROW, NARROW),
        4,
        0.1,
    )


def per_device(tokens, cotangent, inproj_lon, outproj_lon, inproj_lat, outproj_lat, mlp_in, mlp_out):
    core = lax.axis_index("c").astype(jnp.int32).reshape(1)
    pack = jnp.concatenate([tokens, cotangent], axis=2).reshape(TO_LON)
    pack, row_tokens, row_normed, row_packed, row_mixed = call(
        row_forward,
        [(swap(pack, LON), VMEM)] + all_far(inproj_lon, outproj_lon),
        [(TO_TURN, bf16, VMEM)] + far(NARROW, NARROW, QKV, NARROW),
        low(IN, OUT, NARROW, NARROW, QKV, NARROW) + [(NARROW, f32), (NARROW, f32), (TURNED, f32)],
        6,
        5.0,
    )
    pack, normed, mixed, grads, upstream, *saved = call(
        column_both,
        [(swap(pack, TURN), VMEM)] + all_far(inproj_lat, outproj_lat, mlp_in, mlp_out),
        [(TO_TURN, bf16, VMEM)] + far(NARROW, NARROW, QKV, NARROW, NARROW, WIDE, WIDE, NARROW),
        low(IN, OUT, MLP_IN, MLP_OUT, NARROW, NARROW, QKV, NARROW, NARROW, WIDE, WIDE, NARROW, QKV, NARROW)
        + [(TILES, f32), (TILES, f32), (TURNED, f32)] + [(NARROW, f32)] * 4 + [(LAT_PROBS, f32)] * 2,
        12,
        20.0,
    )
    mlp_mine, mlp_other = call(
        mlp_terms,
        [(core, SMEM)] + all_far(*saved),
        far(BY_CHIP, BY_CHIP),
        low(NARROW, WIDE, WIDE, NARROW, HELD, HELD),
        20,
        0.1,
    )
    (mlp,) = call(
        add_cores,
        all_far(mlp_mine, from_other_core(mlp_other)),
        far(BY_CHIP),
        low(BY_CHIP, BY_CHIP),
        12,
        0.1,
    )
    first_sum = lax.psum_scatter(mlp.reshape(FF, WIDTH), "y", scatter_dimension=0, tiled=True)
    lat_mine, lat_other = weight_terms(core, grads, normed, upstream, mixed)
    lat_other = from_other_core(lat_other)
    (weights,) = call(row_weights, all_far(row_packed), far(LON_WEIGHTS), low(QKV, LON_WEIGHTS), 2, 0.1)
    pack, grads, upstream = call(
        row_backward,
        [(swap(pack, TURN), VMEM)] + all_far(row_tokens, row_packed, weights, inproj_lon, outproj_lon),
        [(TO_LON, bf16, VMEM)] + far(QKV, NARROW),
        low(NARROW, QKV, LON_WEIGHTS, IN, OUT, QKV, NARROW) + [(NARROW, f32), (NARROW, f32), (NARROW, bf16)],
        7,
        8.0,
    )
    (first_sum,) = call(
        after_both, all_far(first_sum, upstream), far(first_sum.shape), [], 0, 0.01, {0: 0}
    )
    second_sum = lax.psum_scatter(first_sum, "x", scatter_dimension=0, tiled=True)
    lon_mine, lon_other = weight_terms(core, grads, row_normed, upstream, row_mixed)
    lon_other = from_other_core(lon_other)
    pack = swap(pack, LON).reshape(4, 4, 2 * NEAR, WIDTH).astype(f32)
    (both,) = call(
        join_cores,
        [(lon_mine, VMEM), (lon_other, VMEM), (lat_mine, VMEM), (lat_other, VMEM)],
        [((64, 32, WIDTH), bf16, VMEM)],
        [],
        0,
        0.1,
    )
    rows = jnp.sum(swap(both, CHIPS).astype(f32), axis=0)
    (second_sum,) = call(
        after_both, all_far(second_sum, both), far(second_sum.shape), [], 0, 0.01, {0: 0}
    )
    mlp = jnp.sum(swap(second_sum.reshape(4, 32, WIDTH), ("h", "l")).astype(f32), axis=0)
    return (
        pack[:, :, NEAR:],
        pack[:, :, :NEAR],
        rows[0:12].T,
        rows[12:16].T,
        rows[16:28].T,
        rows[28:32].T,
        mlp[0:16].T,
        mlp[16:32].reshape(4, 4, WIDTH).transpose(0, 2, 1).reshape(FF, 4),
    )


def solution(mesh):
    fine = Mesh(mesh.devices.reshape(4, 2, 4, 2, 2), ("x", "h", "y", "l", "c"))
    grid = P(("x", "h"), None, ("y", "l", "c"), None)
    columns = P(None, ("x", "h", "y", "l", "c"))
    return jax.shard_map(
        per_device,
        mesh=fine,
        in_specs=(grid, grid) + (P(),) * 6,
        out_specs=(grid, grid) + (columns,) * 6,
        check_vma=False,
    )
```

```python
import jax
import jax.numpy as jnp
from jax import lax
from jax.experimental import pallas as pl
from jax.experimental.pallas import tpu as pltpu
from jax.sharding import Mesh, PartitionSpec as P

HEADS = 8
WIDTH = 512
FF = 2048
HEAD = WIDTH // HEADS
SCALE = HEAD**-0.5
EPSILON = 1e-05
ROWS = 352
LATS = 32
NEAR = 22
PART = 11
PIECE = 13
LON = ("y", "l", "c")
TURN = ("y", "x", "h")
CHIPS = ("x", "h", "y", "l")
UNROLL = HEADS // 2
BLOCKS = ((0, 128), (128, 128), (256, 96))
f32 = jnp.float32
bf16 = jnp.bfloat16


def normalize(values):
    center = values - jnp.mean(values, axis=-1, keepdims=True)
    inverse = lax.rsqrt(jnp.mean(center * center, axis=-1, keepdims=True) + EPSILON)
    return center * inverse, inverse


def norm_back(scaled, inverse, upstream):
    return inverse * (
        upstream
        - jnp.mean(upstream, axis=-1, keepdims=True)
        - scaled * jnp.mean(upstream * scaled, axis=-1, keepdims=True)
    )


def dot(left, right, left_dim=1, right_dim=0):
    dims = (((left_dim,), (right_dim,)), ((), ()))
    return lax.dot_general(left, right, dims, preferred_element_type=f32)


def half_of(values, half):
    lanes = lax.broadcasted_iota(jnp.int32, values.shape, 1) // HEAD
    return jnp.where(lanes == half, values, jnp.zeros_like(values))


def pair_columns(part, pair):
    return pl.ds(pl.multiple_of(part * WIDTH + pair * 2 * HEAD, 2 * HEAD), 2 * HEAD)


def over_pairs(body):
    lax.fori_loop(0, HEADS // 2, lambda pair, _: body(pair) or 0, 0, unroll=UNROLL)


def row_probabilities(packed, pair, half):
    keys = half_of(packed[:, pair_columns(1, pair)] * SCALE, half)
    scores = dot(keys, packed[:, pair_columns(0, pair)], 1, 1)
    powers = jnp.exp(scores - jnp.max(scores, axis=0, keepdims=True))
    return (powers * (1.0 / jnp.sum(powers, axis=0, keepdims=True))).astype(bf16)


def put_mixed(turned, pair, half, rows, mixed):
    place = pl.ds(pl.multiple_of(pair * 2 * HEAD + half * HEAD, HEAD), HEAD)
    turned[place, rows] = mixed[half * HEAD : (half + 1) * HEAD]


def put_grads(grads, pair, rows, found):
    for part in range(3):
        both = half_of(found[0][part], 0) + half_of(found[1][part], 1)
        grads[rows, pair_columns(part, pair)] = both.astype(bf16)


def attend_rows(packed, turned):
    def one_pair(pair):
        values = packed[:, pair_columns(2, pair)]
        probs = [row_probabilities(packed, pair, half) for half in range(2)]
        for half in range(2):
            put_mixed(turned, pair, half, pl.ds(0, ROWS), dot(values, probs[half], 0, 0))

    over_pairs(one_pair)


def row_weights(packed_far, after, weights_far, packed, weights, semaphores):
    mover = Mover(semaphores)
    del after
    mover.start(packed_far, packed).wait()

    def one_pair(pair):
        for half in range(2):
            weights[pair * 2 + half] = row_probabilities(packed, pair, half)

    over_pairs(one_pair)
    mover.start(weights, weights_far).wait()


def attend_rows_back(packed, upstream, weights, grads):
    def one_pair(pair):
        queries, keys, values = (packed[:, pair_columns(p, pair)] for p in range(3))
        grad_mix = upstream[:, pair_columns(0, pair)]
        found = []
        for half in range(2):
            low = weights[pair * 2 + half]
            probs = low.astype(f32)
            grad_probs = dot(half_of(values, half), grad_mix, 1, 1)
            inner = jnp.sum(grad_probs * probs, axis=0, keepdims=True)
            grad_scores = (probs * (grad_probs - inner) * SCALE).astype(bf16)
            found.append(
                (dot(grad_scores, keys, 0, 0), dot(grad_scores, queries), dot(low, grad_mix))
            )
        put_grads(grads, pair, pl.ds(0, ROWS), found)

    over_pairs(one_pair)


def column_lanes(count):
    return lax.broadcasted_iota(jnp.int32, (LATS, count), 1) // LATS


def own_columns(square):
    count = square.shape[0]
    lanes = column_lanes(count)
    kept = square[:LATS]
    for column in range(1, count // LATS):
        kept = jnp.where(lanes == column, square[column * LATS : (column + 1) * LATS], kept)
    return kept


def to_square(kept):
    count = kept.shape[1]
    lanes = column_lanes(count)
    parts = [jnp.where(lanes == column, kept, 0.0) for column in range(count // LATS)]
    return jnp.concatenate(parts, axis=0).astype(bf16)


def attend_columns(packed, turned, probs):
    def scores(pair):
        for first, count in BLOCKS:
            rows = pl.ds(first, count)
            queries, keys = (packed[rows, pair_columns(p, pair)] for p in range(2))
            for half in range(2):
                square = dot(half_of(keys * SCALE, half), queries, 1, 1)
                probs[pair * 2 + half, :, rows] = own_columns(square)

    over_pairs(scores)
    powers = probs[...]
    powers = jnp.exp(powers - jnp.max(powers, axis=1, keepdims=True))
    probs[...] = powers * (1.0 / jnp.sum(powers, axis=1, keepdims=True))

    def mix(pair):
        for first, count in BLOCKS:
            rows = pl.ds(first, count)
            values = packed[rows, pair_columns(2, pair)]
            for half in range(2):
                square = to_square(probs[pair * 2 + half, :, rows])
                put_mixed(turned, pair, half, rows, dot(values, square, 0, 0))

    over_pairs(mix)


def attend_columns_back(packed, upstream, probs, grad_scores, grads):
    def products(pair):
        for first, count in BLOCKS:
            rows = pl.ds(first, count)
            values, grad_mix = packed[rows, pair_columns(2, pair)], upstream[rows, pair_columns(0, pair)]
            for half in range(2):
                square = dot(half_of(values, half), grad_mix, 1, 1)
                grad_scores[pair * 2 + half, :, rows] = own_columns(square)

    over_pairs(products)
    grad_probs = grad_scores[...]
    inner = jnp.sum(grad_probs * probs[...], axis=1, keepdims=True)
    grad_scores[...] = probs[...] * (grad_probs - inner) * SCALE

    def combine(pair):
        for first, count in BLOCKS:
            rows = pl.ds(first, count)
            queries, keys = (packed[rows, pair_columns(p, pair)] for p in range(2))
            grad_mix = upstream[rows, pair_columns(0, pair)]
            found = []
            for half in range(2):
                square = to_square(grad_scores[pair * 2 + half, :, rows])
                weights = to_square(probs[pair * 2 + half, :, rows])
                found.append(
                    (dot(square, keys, 0, 0), dot(square, queries), dot(weights, grad_mix))
                )
            put_grads(grads, pair, rows, found)

    over_pairs(combine)


def project(normed, inproj, packed):
    for part in range(3):
        columns = pl.ds(part * WIDTH, WIDTH)
        packed[:, columns] = dot(normed, inproj[:, columns]).astype(bf16)


class Mover:
    def __init__(self, semaphores):
        self.semaphores, self.count = semaphores, 0

    def start(self, source, target):
        copy = pltpu.make_async_copy(source, target, self.semaphores.at[self.count])
        self.count += 1
        copy.start()
        return copy


def row_forward(
    pack, inproj_far, outproj_far,
    out, tokens_far, normed_far, packed_far, mixed_far,
    inproj, outproj, tokens, normed, packed, mixed, hidden, cotangent, turned, semaphores,
):
    mover = Mover(semaphores)
    inproj_in = mover.start(inproj_far, inproj)
    outproj_in = mover.start(outproj_far, outproj)
    for block in range(16):
        piece = pack[block].astype(f32)
        rows = pl.ds(block * NEAR, NEAR)
        hidden[rows, :] = piece[:NEAR]
        cotangent[rows, :] = piece[NEAR:]
    values = hidden[...]
    tokens[...] = values.astype(bf16)
    normed[...] = normalize(values)[0].astype(bf16)
    leaving = [mover.start(tokens, tokens_far), mover.start(normed, normed_far)]
    inproj_in.wait()
    project(normed[...], inproj, packed)
    leaving.append(mover.start(packed, packed_far))
    attend_rows(packed, turned)
    mixed[...] = turned[...].T.astype(bf16)
    leaving.append(mover.start(mixed, mixed_far))
    outproj_in.wait()
    hidden[...] += dot(mixed[...], outproj[...])
    for block in range(LATS):
        rows = pl.ds(block * PART, PART)
        out[block] = jnp.concatenate([hidden[rows, :], cotangent[rows, :]], axis=0).astype(bf16)
    for copy in leaving:
        copy.wait()


def row_backward(
    core, pack, tokens_far, normed_far, packed_far, mixed_far, weights_far, inproj_far, outproj_far,
    out, mine, other,
    tokens, normed, packed, mixed, weights, inproj, outproj, grads, low, hidden, output, upstream, semaphores,
):
    mover = Mover(semaphores)
    outproj_in = mover.start(outproj_far, outproj)
    coming = [mover.start(packed_far, packed), mover.start(weights_far, weights)]
    inproj_in = mover.start(inproj_far, inproj)
    tokens_in = mover.start(tokens_far, tokens)
    last = [mover.start(normed_far, normed), mover.start(mixed_far, mixed)]
    for block in range(LATS):
        piece = pack[block].astype(f32)
        rows = pl.ds(block * PART, PART)
        hidden[rows, :] = piece[:PART]
        output[rows, :] = piece[PART:]
    low[...] = hidden[...].astype(bf16)
    outproj_in.wait()
    upstream[...] = dot(low[...], outproj[...], 1, 1).astype(bf16)
    for copy in coming:
        copy.wait()
    attend_rows_back(packed, upstream, weights, grads)
    inproj_in.wait()
    grad_normed = dot(grads[...], inproj[...], 1, 1)
    tokens_in.wait()
    hidden[...] += norm_back(*normalize(tokens[...].astype(f32)), grad_normed)
    for block in range(16):
        rows = pl.ds(block * NEAR, NEAR)
        out[block] = jnp.concatenate([hidden[rows, :], output[rows, :]], axis=0).astype(bf16)
    for copy in last:
        copy.wait()
    split_terms(core, grads, normed, low, mixed, mine, other)


def to_columns(pack, first, second):
    for lat in range(LATS):
        piece = pack[lat].astype(f32)
        for tile in range(4):
            lanes = slice(tile * 128, (tile + 1) * 128)
            first[tile, pl.ds(lat, PART, stride=LATS), :] = piece[:PART, lanes]
            second[tile, pl.ds(lat, PART, stride=LATS), :] = piece[PART:, lanes]


def joined(tiles):
    return jnp.concatenate([tiles[tile] for tile in range(4)], axis=1)


def put_tiles(tiles, values):
    for tile in range(4):
        tiles[tile] = values[:, tile * 128 : (tile + 1) * 128]


def from_columns(out, first, second):
    for lat in range(LATS):
        rows = pl.ds(lat, PART, stride=LATS)
        parts = [
            jnp.concatenate([tiles[tile, rows, :] for tile in range(4)], axis=1)
            for tiles in (first, second)
        ]
        out[lat] = jnp.concatenate(parts, axis=0).astype(bf16)


def column_both(
    pack, inproj_far, outproj_far, mlp_in_far, mlp_out_far,
    out, normed_far, mixed_far, grads_far, low_far, normed_mlp_far, activated_far, grad_inner_far, cotangent_far,
    inproj, outproj, mlp_in, mlp_out, normed, mixed, grads, low, normed_mlp, activated, grad_inner, cotangent,
    packed, upstream, first, second, turned, hidden_one, hidden, grad_normed, output, probs, grad_scores,
    semaphores,
):
    mover = Mover(semaphores)
    inproj_in = mover.start(inproj_far, inproj)
    outproj_in = mover.start(outproj_far, outproj)
    coming = [mover.start(mlp_in_far, mlp_in), mover.start(mlp_out_far, mlp_out)]
    to_columns(pack, first, second)
    hidden_one[...] = joined(first)
    cotangent[...] = joined(second).astype(bf16)
    normed[...] = normalize(hidden_one[...])[0].astype(bf16)
    leaving = [mover.start(cotangent, cotangent_far), mover.start(normed, normed_far)]
    inproj_in.wait()
    project(normed[...], inproj, packed)
    attend_columns(packed, turned, probs)
    mixed[...] = turned[...].T.astype(bf16)
    leaving.append(mover.start(mixed, mixed_far))
    outproj_in.wait()
    hidden[...] = hidden_one[...] + dot(mixed[...], outproj[...])
    normed_mlp[...] = normalize(hidden[...])[0].astype(bf16)
    leaving.append(mover.start(normed_mlp, normed_mlp_far))
    output[...] = hidden[...]
    grad_normed[...] = jnp.zeros_like(grad_normed)
    for copy in coming:
        copy.wait()

    def one_chunk(chunk, _):
        columns = pl.ds(pl.multiple_of(chunk * 512, 512), 512)
        inner = dot(normed_mlp[...], mlp_in[:, columns])
        spread = 0.5 * (1.0 + lax.erf(inner * 2.0**-0.5))
        slope = spread + inner * (0.5 / jnp.pi) ** 0.5 * jnp.exp(-0.5 * inner * inner)
        active = (inner * spread).astype(bf16)
        activated[:, columns] = active
        output[...] += dot(active, mlp_out[columns, :])
        grad = (dot(cotangent[...], mlp_out[columns, :], 1, 1) * slope).astype(bf16)
        grad_inner[:, columns] = grad
        grad_normed[...] += dot(grad, mlp_in[:, columns], 1, 1)
        return 0

    lax.fori_loop(0, FF // 512, one_chunk, 0, unroll=2)
    leaving.append(mover.start(activated, activated_far))
    leaving.append(mover.start(grad_inner, grad_inner_far))
    put_tiles(second, output[...])
    back = norm_back(*normalize(hidden[...]), grad_normed[...])
    hidden[...] = cotangent[...].astype(f32) + back
    low[...] = hidden[...].astype(bf16)
    leaving.append(mover.start(low, low_far))
    upstream[...] = dot(low[...], outproj[...], 1, 1).astype(bf16)
    attend_columns_back(packed, upstream, probs, grad_scores, grads)
    leaving.append(mover.start(grads, grads_far))
    back = norm_back(*normalize(hidden_one[...]), dot(grads[...], inproj[...], 1, 1))
    put_tiles(first, hidden[...] + back)
    from_columns(out, first, second)
    for copy in leaving:
        copy.wait()


def block_terms(block, grads, normed, low, mixed):
    wide = dot(grads[:, block * 384 : (block + 1) * 384], normed[...], 0, 0)
    slim = dot(low[:, block * 128 : (block + 1) * 128], mixed[...], 0, 0)
    return [wide.reshape(32, 12, WIDTH), slim.reshape(32, 4, WIDTH)]


def column_terms(place, *refs):
    far, mine, others, near, semaphores = refs[:8], refs[8], refs[9:14], refs[14:22], refs[22]
    mover = Mover(semaphores)
    coming = [mover.start(source, target) for source, target in zip(far, near)]
    normed_mlp, activated, grad_inner, cotangent, grads, normed, low, mixed = near
    for copy in coming:
        copy.wait()
    for block in range(4):
        terms = block_terms(block, grads, normed, low, mixed)
        inner = dot(grad_inner[:, block * 512 : (block + 1) * 512], normed_mlp[...], 0, 0)
        outer = dot(cotangent[:, block * 128 : (block + 1) * 128], activated[...], 0, 0)
        terms.append(inner.reshape(32, 16, WIDTH))
        for part in range(4):
            terms.append(outer[:, part * WIDTH : (part + 1) * WIDTH].reshape(32, 4, WIDTH))
        both = jnp.concatenate(terms, axis=1).astype(bf16).reshape(2, 4, 2, 2, 48, WIDTH)
        for high in range(2):
            even, odd = both[high, :, :, 0], both[high, :, :, 1]
            mine[block, :, high] = jnp.where(place[0] == 0, even, odd)
            leaving = jnp.where(place[0] == 0, odd, even)
            for row in range(4):
                for low_z in range(2):
                    piece, chip = divmod(16 * block + 4 * row + 2 * high + low_z, PIECE)
                    others[piece][chip] = leaving[row, low_z]


def split_terms(place, grads, normed, low, mixed, mine, other):
    for block in range(4):
        terms = jnp.concatenate(block_terms(block, grads, normed, low, mixed), axis=1)
        terms = terms.astype(bf16).reshape(16, 2, 16, WIDTH)
        chips = pl.ds(block * 16, 16)
        mine[chips] = jnp.where(place[0] == 0, terms[:, 0], terms[:, 1])
        other[chips] = jnp.where(place[0] == 0, terms[:, 1], terms[:, 0])


def join_cores(mine, other, out):
    for block in range(4):
        chips = pl.ds(block * 16, 16)
        out[chips] = (mine[chips].astype(f32) + other[chips].astype(f32)).astype(bf16)


def add_cores(mine, *refs):
    others, out_far, total, semaphores = refs[:5], *refs[5:]
    mover = Mover(semaphores)
    leaving = []
    for block in range(4):
        for place in range(16):
            row, rest = divmod(place, 4)
            high, low_z = divmod(rest, 2)
            piece, chip = divmod(16 * block + place, PIECE)
            own = mine[block, row, high, low_z].astype(f32)
            total[block, row, high, low_z] = (own + others[piece][chip].astype(f32)).astype(bf16)
        leaving.append(mover.start(total.at[block], out_far.at[block]))
    for copy in leaving:
        copy.wait()


def sum_row(parts, lon_in, lon_out):
    total = jnp.sum(parts[...].astype(f32), axis=0)
    lon_in[...] = total[0:12]
    lon_out[...] = total[12:16]


def pick_y(place, blocks, *outs):
    for step in range(4):
        outs[step][...] = blocks[jnp.bitwise_xor(place[1], step)]


def sum_pick_z(place, *refs):
    parts, outs, total = refs[:4], refs[4:8], refs[8]
    added = sum(part[...].astype(f32) for part in parts)
    total[...] = added.astype(bf16).reshape(total.shape)
    for step in range(4):
        outs[step][...] = total[jnp.bitwise_xor(place[2], step)]


def sum_column(*refs):
    parts, (lat_in, lat_out, wide_in, wide_out) = refs[:4], refs[4:]
    total = sum(part[...].astype(f32) for part in parts)
    lat_in[...] = total[0:12]
    lat_out[...] = total[12:16]
    wide_in[...] = total[16:32]
    for part in range(4):
        wide_out[:, part * WIDTH : (part + 1) * WIDTH] = total[32 + 4 * part : 36 + 4 * part]


SMEM, VMEM, HBM = pltpu.SMEM, pltpu.VMEM, pltpu.HBM


def call(kernel, args, outs, scratch, semaphores, megabytes, gigaflops, aliases=None):
    arrays = [
        pltpu.with_memory_space_constraint(array, HBM) if place is HBM else array
        for array, place in args
    ]
    scratch = [pltpu.VMEM(shape, kind) for shape, kind in scratch]
    if semaphores:
        scratch.append(pltpu.SemaphoreType.DMA((semaphores,)))
    return pl.pallas_call(
        kernel,
        out_shape=[
            jax.ShapeDtypeStruct(shape, kind) if place is pl.ANY else place(shape, kind)
            for shape, kind, place in outs
        ],
        in_specs=[pl.BlockSpec(memory_space=place) for _, place in args],
        out_specs=[
            pl.BlockSpec(memory_space=VMEM if place is pl.ANY else place) for _, _, place in outs
        ],
        scratch_shapes=scratch,
        compiler_params=pltpu.CompilerParams(vmem_limit_bytes=megabytes << 20),
        cost_estimate=pl.CostEstimate(
            flops=int(gigaflops * 1e9), bytes_accessed=1 << 16, transcendentals=0
        ),
        input_output_aliases=aliases or {},
    )(*arrays)


def swap(array, axes):
    return lax.all_to_all(array, axes, split_axis=0, concat_axis=0, tiled=True)


def trade(parts, axes):
    moved = [
        lax.ppermute(part, axes, [(place, place ^ step) for place in range(4)])
        for step, part in enumerate(parts)
        if step
    ]
    return [parts[0], *moved]


def from_other_core(array):
    return lax.ppermute(array, "c", [(0, 1), (1, 0)])


NARROW = (ROWS, WIDTH)
QKV = (ROWS, 3 * WIDTH)
WIDE = (ROWS, FF)
TILES = (4, ROWS, 128)
TURNED = (WIDTH, ROWS)
TO_TURN = (LATS, 2 * PART, WIDTH)
TO_LON = (16, 2 * NEAR, WIDTH)
LON_WEIGHTS = (HEADS, ROWS, ROWS)
LAT_PROBS = (HEADS, LATS, ROWS)
IN, OUT, MLP_IN, MLP_OUT = (WIDTH, 3 * WIDTH), (WIDTH, WIDTH), (WIDTH, FF), (FF, WIDTH)
SUMS = (64, 16, WIDTH)
BY_CHIP = (4, 4, 2, 2, 48, WIDTH)


def low(*shapes):
    return [(shape, bf16) for shape in shapes]


def far(*shapes):
    return [(shape, bf16, HBM) for shape in shapes]


def all_far(*arrays):
    return [(array, HBM) for array in arrays]


def per_device(tokens, cotangent, inproj_lon, outproj_lon, inproj_lat, outproj_lat, mlp_in, mlp_out):
    core = jnp.stack([lax.axis_index(axes) for axes in ("c", "y", ("h", "l"))]).astype(jnp.int32)
    pack = jnp.concatenate([tokens, cotangent], axis=2).reshape(TO_LON)
    pack, row_tokens, row_normed, row_packed, row_mixed = call(
        row_forward,
        [(swap(pack, LON), VMEM)] + all_far(inproj_lon, outproj_lon),
        [(TO_TURN, bf16, VMEM)] + far(NARROW, NARROW, QKV, NARROW),
        low(IN, OUT, NARROW, NARROW, QKV, NARROW) + [(NARROW, f32), (NARROW, f32), (TURNED, f32)],
        6,
        20,
        5.0,
    )
    pack, normed, mixed, grads, upstream, *saved = call(
        column_both,
        [(swap(pack, TURN), VMEM)] + all_far(inproj_lat, outproj_lat, mlp_in, mlp_out),
        [(TO_TURN, bf16, VMEM)] + far(NARROW, NARROW, QKV, NARROW, NARROW, WIDE, WIDE, NARROW),
        low(IN, OUT, MLP_IN, MLP_OUT, NARROW, NARROW, QKV, NARROW, NARROW, WIDE, WIDE, NARROW, QKV, NARROW)
        + [(TILES, f32), (TILES, f32), (TURNED, f32)] + [(NARROW, f32)] * 4 + [(LAT_PROBS, f32)] * 2,
        12,
        36,
        20.0,
    )
    mine, *others = call(
        column_terms,
        [(core, SMEM)] + all_far(*saved, grads, normed, upstream, mixed),
        [(BY_CHIP, bf16, VMEM)] + [((PIECE, 48, WIDTH), bf16, VMEM)] * 5,
        low(NARROW, WIDE, WIDE, NARROW, QKV, NARROW, NARROW, NARROW),
        8,
        32,
        0.1,
    )
    (weights,) = call(
        row_weights,
        [(row_packed, HBM), (mine, pl.ANY)],
        far(LON_WEIGHTS),
        low(QKV, LON_WEIGHTS),
        2,
        12,
        0.1,
    )
    (column,) = call(
        add_cores,
        [(mine, VMEM)] + [(from_other_core(other), VMEM) for other in others],
        far(BY_CHIP),
        low(BY_CHIP),
        4,
        20,
        0.1,
    )
    column = lax.psum_scatter(column.reshape(3072, WIDTH), "x", scatter_dimension=0, tiled=True)
    pack, lon_mine, lon_other = call(
        row_backward,
        [(core, SMEM), (swap(pack, TURN), VMEM)]
        + all_far(row_tokens, row_normed, row_packed, row_mixed, weights, inproj_lon, outproj_lon),
        [(TO_LON, bf16, VMEM), (SUMS, bf16, VMEM), (SUMS, bf16, VMEM)],
        low(NARROW, NARROW, QKV, NARROW, LON_WEIGHTS, IN, OUT, QKV, NARROW)
        + [(NARROW, f32), (NARROW, f32), (NARROW, bf16)],
        7,
        28,
        60.0,
    )
    lon_other = from_other_core(lon_other)
    pack = swap(pack, LON)
    (both,) = call(
        join_cores, [(lon_mine, VMEM), (lon_other, VMEM)], [(SUMS, bf16, VMEM)], [], 0, 12, 0.1
    )
    unpacked = pack.reshape(4, 4, 2 * NEAR, WIDTH).astype(f32)
    lon = call(
        sum_row,
        [(swap(both, CHIPS), VMEM)],
        [((12, WIDTH), f32, pl.ANY), ((4, WIDTH), f32, pl.ANY)],
        [],
        0,
        12,
        60.0,
    )
    parts = call(
        pick_y,
        [(core, SMEM), (column.reshape(4, 192, WIDTH), VMEM)],
        [((192, WIDTH), bf16, VMEM)] * 4,
        [],
        0,
        8,
        0.01,
    )
    parts = call(
        sum_pick_z,
        [(core, SMEM)] + [(part, VMEM) for part in trade(parts, "y")],
        [((48, WIDTH), bf16, VMEM)] * 4,
        low((4, 48, WIDTH)),
        0,
        8,
        0.01,
    )
    column = call(
        sum_column,
        [(part, VMEM) for part in trade(parts, ("h", "l"))],
        [((rows, lanes), f32, pl.ANY) for rows, lanes in ((12, WIDTH), (4, WIDTH), (16, WIDTH), (4, FF))],
        [],
        0,
        4,
        0.1,
    )
    return (
        unpacked[:, :, NEAR:],
        unpacked[:, :, :NEAR],
        *(array.T for array in lon),
        *(array.T for array in column),
    )


def solution(mesh):
    fine = Mesh(mesh.devices.reshape(4, 2, 4, 2, 2), ("x", "h", "y", "l", "c"))
    grid = P(("x", "h"), None, ("y", "l", "c"), None)
    columns = P(None, ("x", "h", "y", "l", "c"))
    return jax.shard_map(
        per_device,
        mesh=fine,
        in_specs=(grid, grid) + (P(),) * 6,
        out_specs=(grid, grid) + (columns,) * 6,
        check_vma=False,
    )
```

```python
import jax
import jax.numpy as jnp
from jax import lax
from jax.experimental import pallas as pl
from jax.experimental.pallas import tpu as pltpu
from jax.sharding import Mesh, PartitionSpec as P

HEADS = 8
WIDTH = 512
FF = 2048
HEAD = WIDTH // HEADS
SCALE = HEAD**-0.5
EPSILON = 1e-05
ROWS = 352
LATS = 32
NEAR = 22
PART = 11
PIECE = 13
LON = ("y", "l", "c")
TURN = ("h", "x", "y")
CHIPS = ("x", "h", "y", "l")
UNROLL = HEADS // 2
BLOCKS = ((0, 128), (128, 128), (256, 96))
f32 = jnp.float32
bf16 = jnp.bfloat16


def normalize(values):
    center = values - jnp.mean(values, axis=-1, keepdims=True)
    inverse = lax.rsqrt(jnp.mean(center * center, axis=-1, keepdims=True) + EPSILON)
    return center * inverse, inverse


def norm_back(scaled, inverse, upstream):
    return inverse * (
        upstream
        - jnp.mean(upstream, axis=-1, keepdims=True)
        - scaled * jnp.mean(upstream * scaled, axis=-1, keepdims=True)
    )


def dot(left, right, left_dim=1, right_dim=0):
    dims = (((left_dim,), (right_dim,)), ((), ()))
    return lax.dot_general(left, right, dims, preferred_element_type=f32)


def half_of(values, half):
    lanes = lax.broadcasted_iota(jnp.int32, values.shape, 1) // HEAD
    return jnp.where(lanes == half, values, jnp.zeros_like(values))


def pair_columns(part, pair):
    return pl.ds(pl.multiple_of(part * WIDTH + pair * 2 * HEAD, 2 * HEAD), 2 * HEAD)


def over_pairs(body):
    lax.fori_loop(0, HEADS // 2, lambda pair, _: body(pair) or 0, 0, unroll=UNROLL)


def row_probabilities(packed, pair, half):
    keys = half_of(packed[:, pair_columns(1, pair)] * SCALE, half)
    scores = dot(keys, packed[:, pair_columns(0, pair)], 1, 1)
    powers = jnp.exp(scores - jnp.max(scores, axis=0, keepdims=True))
    return (powers * (1.0 / jnp.sum(powers, axis=0, keepdims=True))).astype(bf16)


def put_mixed(turned, pair, half, rows, mixed):
    place = pl.ds(pl.multiple_of(pair * 2 * HEAD + half * HEAD, HEAD), HEAD)
    turned[place, rows] = mixed[half * HEAD : (half + 1) * HEAD]


def put_grads(grads, pair, rows, found):
    for part in range(3):
        both = half_of(found[0][part], 0) + half_of(found[1][part], 1)
        grads[rows, pair_columns(part, pair)] = both.astype(bf16)


def attend_rows(packed, turned):
    def one_pair(pair):
        values = packed[:, pair_columns(2, pair)]
        probs = [row_probabilities(packed, pair, half) for half in range(2)]
        for half in range(2):
            put_mixed(turned, pair, half, pl.ds(0, ROWS), dot(values, probs[half], 0, 0))

    over_pairs(one_pair)


def row_weights(packed_far, after, weights_far, packed, weights, semaphores):
    mover = Mover(semaphores)
    del after
    mover.start(packed_far, packed).wait()

    def one_pair(pair):
        for half in range(2):
            weights[pair * 2 + half] = row_probabilities(packed, pair, half)

    over_pairs(one_pair)
    mover.start(weights, weights_far).wait()


def attend_rows_back(packed, upstream, weights, grads):
    def one_pair(pair):
        queries, keys, values = (packed[:, pair_columns(p, pair)] for p in range(3))
        grad_mix = upstream[:, pair_columns(0, pair)]
        found = []
        for half in range(2):
            low = weights[pair * 2 + half]
            probs = low.astype(f32)
            grad_probs = dot(half_of(values, half), grad_mix, 1, 1)
            inner = jnp.sum(grad_probs * probs, axis=0, keepdims=True)
            grad_scores = (probs * (grad_probs - inner) * SCALE).astype(bf16)
            found.append(
                (dot(grad_scores, keys, 0, 0), dot(grad_scores, queries), dot(low, grad_mix))
            )
        put_grads(grads, pair, pl.ds(0, ROWS), found)

    over_pairs(one_pair)


def column_lanes(count):
    return lax.broadcasted_iota(jnp.int32, (LATS, count), 1) // LATS


def own_columns(square):
    count = square.shape[0]
    lanes = column_lanes(count)
    kept = square[:LATS]
    for column in range(1, count // LATS):
        kept = jnp.where(lanes == column, square[column * LATS : (column + 1) * LATS], kept)
    return kept


def to_square(kept):
    count = kept.shape[1]
    lanes = column_lanes(count)
    parts = [jnp.where(lanes == column, kept, 0.0) for column in range(count // LATS)]
    return jnp.concatenate(parts, axis=0).astype(bf16)


def attend_columns(packed, turned, probs):
    def scores(pair):
        for first, count in BLOCKS:
            rows = pl.ds(first, count)
            queries, keys = (packed[rows, pair_columns(p, pair)] for p in range(2))
            for half in range(2):
                square = dot(half_of(keys * SCALE, half), queries, 1, 1)
                probs[pair * 2 + half, :, rows] = own_columns(square)

    over_pairs(scores)
    powers = probs[...]
    powers = jnp.exp(powers - jnp.max(powers, axis=1, keepdims=True))
    probs[...] = powers * (1.0 / jnp.sum(powers, axis=1, keepdims=True))

    def mix(pair):
        for first, count in BLOCKS:
            rows = pl.ds(first, count)
            values = packed[rows, pair_columns(2, pair)]
            for half in range(2):
                square = to_square(probs[pair * 2 + half, :, rows])
                put_mixed(turned, pair, half, rows, dot(values, square, 0, 0))

    over_pairs(mix)


def attend_columns_back(packed, upstream, probs, grad_scores, grads):
    def products(pair):
        for first, count in BLOCKS:
            rows = pl.ds(first, count)
            values, grad_mix = packed[rows, pair_columns(2, pair)], upstream[rows, pair_columns(0, pair)]
            for half in range(2):
                square = dot(half_of(values, half), grad_mix, 1, 1)
                grad_scores[pair * 2 + half, :, rows] = own_columns(square)

    over_pairs(products)
    grad_probs = grad_scores[...]
    inner = jnp.sum(grad_probs * probs[...], axis=1, keepdims=True)
    grad_scores[...] = probs[...] * (grad_probs - inner) * SCALE

    def combine(pair):
        for first, count in BLOCKS:
            rows = pl.ds(first, count)
            queries, keys = (packed[rows, pair_columns(p, pair)] for p in range(2))
            grad_mix = upstream[rows, pair_columns(0, pair)]
            found = []
            for half in range(2):
                square = to_square(grad_scores[pair * 2 + half, :, rows])
                weights = to_square(probs[pair * 2 + half, :, rows])
                found.append(
                    (dot(square, keys, 0, 0), dot(square, queries), dot(weights, grad_mix))
                )
            put_grads(grads, pair, rows, found)

    over_pairs(combine)


def project(normed, inproj, packed):
    for part in range(3):
        columns = pl.ds(part * WIDTH, WIDTH)
        packed[:, columns] = dot(normed, inproj[:, columns]).astype(bf16)


class Mover:
    def __init__(self, semaphores):
        self.semaphores, self.count = semaphores, 0

    def start(self, source, target):
        copy = pltpu.make_async_copy(source, target, self.semaphores.at[self.count])
        self.count += 1
        copy.start()
        return copy


def row_forward(
    pack, inproj_far, outproj_far,
    out, tokens_far, normed_far, packed_far, mixed_far,
    inproj, outproj, tokens, normed, packed, mixed, hidden, cotangent, turned, semaphores,
):
    mover = Mover(semaphores)
    inproj_in = mover.start(inproj_far, inproj)
    outproj_in = mover.start(outproj_far, outproj)
    for block in range(16):
        piece = pack[block].astype(f32)
        rows = pl.ds(block * NEAR, NEAR)
        hidden[rows, :] = piece[:NEAR]
        cotangent[rows, :] = piece[NEAR:]
    values = hidden[...]
    tokens[...] = values.astype(bf16)
    normed[...] = normalize(values)[0].astype(bf16)
    leaving = [mover.start(tokens, tokens_far), mover.start(normed, normed_far)]
    inproj_in.wait()
    project(normed[...], inproj, packed)
    leaving.append(mover.start(packed, packed_far))
    attend_rows(packed, turned)
    mixed[...] = turned[...].T.astype(bf16)
    leaving.append(mover.start(mixed, mixed_far))
    outproj_in.wait()
    hidden[...] += dot(mixed[...], outproj[...])
    for block in range(LATS):
        rows = pl.ds(block * PART, PART)
        out[block] = jnp.concatenate([hidden[rows, :], cotangent[rows, :]], axis=0).astype(bf16)
    for copy in leaving:
        copy.wait()


def row_backward(
    core, pack, tokens_far, normed_far, packed_far, mixed_far, weights_far, inproj_far, outproj_far,
    out, mine, other,
    tokens, normed, packed, mixed, weights, inproj, outproj, grads, low, hidden, output, upstream, semaphores,
):
    mover = Mover(semaphores)
    outproj_in = mover.start(outproj_far, outproj)
    coming = [mover.start(packed_far, packed), mover.start(weights_far, weights)]
    inproj_in = mover.start(inproj_far, inproj)
    tokens_in = mover.start(tokens_far, tokens)
    last = [mover.start(normed_far, normed), mover.start(mixed_far, mixed)]
    for block in range(LATS):
        piece = pack[block].astype(f32)
        rows = pl.ds(block * PART, PART)
        hidden[rows, :] = piece[:PART]
        output[rows, :] = piece[PART:]
    low[...] = hidden[...].astype(bf16)
    outproj_in.wait()
    upstream[...] = dot(low[...], outproj[...], 1, 1).astype(bf16)
    for copy in coming:
        copy.wait()
    attend_rows_back(packed, upstream, weights, grads)
    inproj_in.wait()
    grad_normed = dot(grads[...], inproj[...], 1, 1)
    tokens_in.wait()
    hidden[...] += norm_back(*normalize(tokens[...].astype(f32)), grad_normed)
    for block in range(16):
        rows = pl.ds(block * NEAR, NEAR)
        out[block] = jnp.concatenate([hidden[rows, :], output[rows, :]], axis=0).astype(bf16)
    for copy in last:
        copy.wait()
    split_terms(core, grads, normed, low, mixed, mine, other)


def to_columns(pack, columns):
    for lat in range(LATS):
        piece = pack[lat].astype(f32)
        for tile in range(4):
            lanes = slice(tile * 128, (tile + 1) * 128)
            columns[tile, pl.ds(lat, 2 * PART, stride=LATS), :] = piece[:, lanes]


def joined(columns, unit):
    rows = pl.ds(unit * ROWS, ROWS)
    return jnp.concatenate([columns[tile, rows, :] for tile in range(4)], axis=1)


def put_columns(columns, unit, values):
    for tile in range(4):
        columns[tile, pl.ds(unit * ROWS, ROWS), :] = values[:, tile * 128 : (tile + 1) * 128]


def from_columns(out, columns):
    for lat in range(LATS):
        rows = pl.ds(lat, 2 * PART, stride=LATS)
        piece = jnp.concatenate([columns[tile, rows, :] for tile in range(4)], axis=1)
        out[lat] = piece.astype(bf16)


def column_both(
    pack, inproj_far, outproj_far, mlp_in_far, mlp_out_far,
    out, normed_far, mixed_far, grads_far, low_far, normed_mlp_far, activated_far, grad_inner_far, cotangent_far,
    inproj, outproj, mlp_in, mlp_out, normed, mixed, grads, low, normed_mlp, activated, grad_inner, cotangent,
    packed, upstream, columns, turned, hidden_one, hidden, grad_normed, output, probs, grad_scores,
    semaphores,
):
    mover = Mover(semaphores)
    inproj_in = mover.start(inproj_far, inproj)
    outproj_in = mover.start(outproj_far, outproj)
    coming = [mover.start(mlp_in_far, mlp_in), mover.start(mlp_out_far, mlp_out)]
    to_columns(pack, columns)
    hidden_one[...] = joined(columns, 0)
    cotangent[...] = joined(columns, 1).astype(bf16)
    normed[...] = normalize(hidden_one[...])[0].astype(bf16)
    leaving = [mover.start(cotangent, cotangent_far), mover.start(normed, normed_far)]
    inproj_in.wait()
    project(normed[...], inproj, packed)
    attend_columns(packed, turned, probs)
    mixed[...] = turned[...].T.astype(bf16)
    leaving.append(mover.start(mixed, mixed_far))
    outproj_in.wait()
    hidden[...] = hidden_one[...] + dot(mixed[...], outproj[...])
    normed_mlp[...] = normalize(hidden[...])[0].astype(bf16)
    leaving.append(mover.start(normed_mlp, normed_mlp_far))
    output[...] = hidden[...]
    grad_normed[...] = jnp.zeros_like(grad_normed)
    for copy in coming:
        copy.wait()

    def one_chunk(chunk, _):
        chosen = pl.ds(pl.multiple_of(chunk * 512, 512), 512)
        inner = dot(normed_mlp[...], mlp_in[:, chosen])
        spread = 0.5 * (1.0 + lax.erf(inner * 2.0**-0.5))
        slope = spread + inner * (0.5 / jnp.pi) ** 0.5 * jnp.exp(-0.5 * inner * inner)
        active = (inner * spread).astype(bf16)
        activated[:, chosen] = active
        output[...] += dot(active, mlp_out[chosen, :])
        grad = (dot(cotangent[...], mlp_out[chosen, :], 1, 1) * slope).astype(bf16)
        grad_inner[:, chosen] = grad
        grad_normed[...] += dot(grad, mlp_in[:, chosen], 1, 1)
        return 0

    lax.fori_loop(0, FF // 512, one_chunk, 0, unroll=4)
    leaving.append(mover.start(activated, activated_far))
    leaving.append(mover.start(grad_inner, grad_inner_far))
    put_columns(columns, 1, output[...])
    back = norm_back(*normalize(hidden[...]), grad_normed[...])
    hidden[...] = cotangent[...].astype(f32) + back
    low[...] = hidden[...].astype(bf16)
    leaving.append(mover.start(low, low_far))
    upstream[...] = dot(low[...], outproj[...], 1, 1).astype(bf16)
    attend_columns_back(packed, upstream, probs, grad_scores, grads)
    leaving.append(mover.start(grads, grads_far))
    back = norm_back(*normalize(hidden_one[...]), dot(grads[...], inproj[...], 1, 1))
    put_columns(columns, 0, hidden[...] + back)
    from_columns(out, columns)
    for copy in leaving:
        copy.wait()


def block_terms(block, grads, normed, low, mixed):
    wide = dot(grads[:, block * 384 : (block + 1) * 384], normed[...], 0, 0)
    slim = dot(low[:, block * 128 : (block + 1) * 128], mixed[...], 0, 0)
    return [wide.reshape(32, 12, WIDTH), slim.reshape(32, 4, WIDTH)]


def put_terms(place, terms, block, rows, mine, others):
    both = jnp.concatenate(terms, axis=1).astype(bf16)
    both = both.reshape(2, 4, 2, 2, both.shape[1], WIDTH)
    for high in range(2):
        even, odd = both[high, :, :, 0], both[high, :, :, 1]
        mine[block, :, high, :, rows, :] = jnp.where(place[0] == 0, even, odd)
        leaving = jnp.where(place[0] == 0, odd, even)
        for row in range(4):
            for low_z in range(2):
                piece, chip = divmod(16 * block + 4 * row + 2 * high + low_z, PIECE)
                others[piece][chip, rows, :] = leaving[row, low_z]


def column_terms(place, *refs):
    far, mine, others, near, semaphores = refs[:8], refs[8], refs[9:14], refs[14:22], refs[22]
    mover = Mover(semaphores)
    coming = [mover.start(source, target) for source, target in zip(far, near)]
    grads, normed, low, mixed, normed_mlp, grad_inner, activated, cotangent = near
    for copy in coming[:4]:
        copy.wait()
    for block in range(4):
        terms = block_terms(block, grads, normed, low, mixed)
        put_terms(place, terms, block, pl.ds(0, 16), mine, others)
    for copy in coming[4:]:
        copy.wait()
    for block in range(4):
        inner = dot(grad_inner[:, block * 512 : (block + 1) * 512], normed_mlp[...], 0, 0)
        outer = dot(cotangent[:, block * 128 : (block + 1) * 128], activated[...], 0, 0)
        terms = [inner.reshape(32, 16, WIDTH)]
        for part in range(4):
            terms.append(outer[:, part * WIDTH : (part + 1) * WIDTH].reshape(32, 4, WIDTH))
        put_terms(place, terms, block, pl.ds(16, 32), mine, others)


def split_terms(place, grads, normed, low, mixed, mine, other):
    for block in range(4):
        terms = jnp.concatenate(block_terms(block, grads, normed, low, mixed), axis=1)
        terms = terms.astype(bf16).reshape(16, 2, 16, WIDTH)
        chips = pl.ds(block * 16, 16)
        mine[chips] = jnp.where(place[0] == 0, terms[:, 0], terms[:, 1])
        other[chips] = jnp.where(place[0] == 0, terms[:, 1], terms[:, 0])


def join_cores(mine, other, out):
    for block in range(4):
        chips = pl.ds(block * 16, 16)
        out[chips] = (mine[chips].astype(f32) + other[chips].astype(f32)).astype(bf16)


def add_cores(mine, *refs):
    others, out_far, total, semaphores = refs[:5], *refs[5:]
    mover = Mover(semaphores)
    leaving = []
    for block in range(4):
        for place in range(16):
            row, rest = divmod(place, 4)
            high, low_z = divmod(rest, 2)
            piece, chip = divmod(16 * block + place, PIECE)
            own = mine[block, row, high, low_z].astype(f32)
            total[block, row, high, low_z] = (own + others[piece][chip].astype(f32)).astype(bf16)
        leaving.append(mover.start(total.at[block], out_far.at[block]))
    for copy in leaving:
        copy.wait()


def sum_row(parts, lon_in, lon_out):
    total = jnp.sum(parts[...].astype(f32), axis=0)
    lon_in[...] = total[0:12]
    lon_out[...] = total[12:16]


def pick_y(place, blocks, *outs):
    for step in range(4):
        outs[step][...] = blocks[jnp.bitwise_xor(place[1], step)]


def sum_pick_z(place, *refs):
    parts, outs, total = refs[:4], refs[4:8], refs[8]
    added = sum(part[...].astype(f32) for part in parts)
    total[...] = added.astype(bf16).reshape(total.shape)
    for step in range(4):
        outs[step][...] = total[jnp.bitwise_xor(place[2], step)]


def sum_column(*refs):
    parts, (lat_in, lat_out, wide_in, wide_out) = refs[:4], refs[4:]
    total = sum(part[...].astype(f32) for part in parts)
    lat_in[...] = total[0:12]
    lat_out[...] = total[12:16]
    wide_in[...] = total[16:32]
    for part in range(4):
        wide_out[:, part * WIDTH : (part + 1) * WIDTH] = total[32 + 4 * part : 36 + 4 * part]


SMEM, VMEM, HBM = pltpu.SMEM, pltpu.VMEM, pltpu.HBM


def call(kernel, args, outs, scratch, semaphores, megabytes, gigaflops, aliases=None):
    arrays = [
        pltpu.with_memory_space_constraint(array, HBM) if place is HBM else array
        for array, place in args
    ]
    scratch = [pltpu.VMEM(shape, kind) for shape, kind in scratch]
    if semaphores:
        scratch.append(pltpu.SemaphoreType.DMA((semaphores,)))
    return pl.pallas_call(
        kernel,
        out_shape=[
            jax.ShapeDtypeStruct(shape, kind) if place is pl.ANY else place(shape, kind)
            for shape, kind, place in outs
        ],
        in_specs=[pl.BlockSpec(memory_space=place) for _, place in args],
        out_specs=[
            pl.BlockSpec(memory_space=VMEM if place is pl.ANY else place) for _, _, place in outs
        ],
        scratch_shapes=scratch,
        compiler_params=pltpu.CompilerParams(vmem_limit_bytes=megabytes << 20),
        cost_estimate=pl.CostEstimate(
            flops=int(gigaflops * 1e9), bytes_accessed=1 << 16, transcendentals=0
        ),
        input_output_aliases=aliases or {},
    )(*arrays)


def swap(array, axes):
    return lax.all_to_all(array, axes, split_axis=0, concat_axis=0, tiled=True)


def trade(parts, axes):
    moved = [
        lax.ppermute(part, axes, [(place, place ^ step) for place in range(4)])
        for step, part in enumerate(parts)
        if step
    ]
    return [parts[0], *moved]


def from_other_core(array):
    return lax.ppermute(array, "c", [(0, 1), (1, 0)])


NARROW = (ROWS, WIDTH)
QKV = (ROWS, 3 * WIDTH)
WIDE = (ROWS, FF)
TILES = (4, 2 * ROWS, 128)
TURNED = (WIDTH, ROWS)
TO_TURN = (LATS, 2 * PART, WIDTH)
TO_LON = (16, 2 * NEAR, WIDTH)
LON_WEIGHTS = (HEADS, ROWS, ROWS)
LAT_PROBS = (HEADS, LATS, ROWS)
IN, OUT, MLP_IN, MLP_OUT = (WIDTH, 3 * WIDTH), (WIDTH, WIDTH), (WIDTH, FF), (FF, WIDTH)
SUMS = (64, 16, WIDTH)
BY_CHIP = (4, 4, 2, 2, 48, WIDTH)


def low(*shapes):
    return [(shape, bf16) for shape in shapes]


def far(*shapes):
    return [(shape, bf16, HBM) for shape in shapes]


def all_far(*arrays):
    return [(array, HBM) for array in arrays]


def per_device(tokens, cotangent, inproj_lon, outproj_lon, inproj_lat, outproj_lat, mlp_in, mlp_out):
    core = jnp.stack([lax.axis_index(axes) for axes in ("c", "y", ("h", "l"))]).astype(jnp.int32)
    pack = jnp.concatenate([tokens, cotangent], axis=2).reshape(TO_LON)
    pack, row_tokens, row_normed, row_packed, row_mixed = call(
        row_forward,
        [(swap(pack, LON), VMEM)] + all_far(inproj_lon, outproj_lon),
        [(TO_TURN, bf16, VMEM)] + far(NARROW, NARROW, QKV, NARROW),
        low(IN, OUT, NARROW, NARROW, QKV, NARROW) + [(NARROW, f32), (NARROW, f32), (TURNED, f32)],
        6,
        20,
        5.0,
    )
    pack, normed, mixed, grads, upstream, *saved = call(
        column_both,
        [(swap(pack, TURN), VMEM)] + all_far(inproj_lat, outproj_lat, mlp_in, mlp_out),
        [(TO_TURN, bf16, VMEM)] + far(NARROW, NARROW, QKV, NARROW, NARROW, WIDE, WIDE, NARROW),
        low(IN, OUT, MLP_IN, MLP_OUT, NARROW, NARROW, QKV, NARROW, NARROW, WIDE, WIDE, NARROW, QKV, NARROW)
        + [(TILES, f32), (TURNED, f32)] + [(NARROW, f32)] * 4 + [(LAT_PROBS, f32)] * 2,
        12,
        36,
        20.0,
    )
    mine, *others = call(
        column_terms,
        [(core, SMEM)] + all_far(grads, normed, upstream, mixed, *(saved[i] for i in (0, 2, 1, 3))),
        [(BY_CHIP, bf16, VMEM)] + [((PIECE, 48, WIDTH), bf16, VMEM)] * 5,
        low(QKV, NARROW, NARROW, NARROW, NARROW, WIDE, WIDE, NARROW),
        8,
        32,
        0.1,
    )
    (weights,) = call(
        row_weights,
        [(row_packed, HBM), (mine, pl.ANY)],
        far(LON_WEIGHTS),
        low(QKV, LON_WEIGHTS),
        2,
        12,
        0.1,
    )
    (column,) = call(
        add_cores,
        [(mine, VMEM)] + [(from_other_core(other), VMEM) for other in others],
        far(BY_CHIP),
        low(BY_CHIP),
        4,
        20,
        0.1,
    )
    column = lax.psum_scatter(column.reshape(3072, WIDTH), "x", scatter_dimension=0, tiled=True)
    pack, lon_mine, lon_other = call(
        row_backward,
        [(core, SMEM), (swap(pack, TURN), VMEM)]
        + all_far(row_tokens, row_normed, row_packed, row_mixed, weights, inproj_lon, outproj_lon),
        [(TO_LON, bf16, VMEM), (SUMS, bf16, VMEM), (SUMS, bf16, VMEM)],
        low(NARROW, NARROW, QKV, NARROW, LON_WEIGHTS, IN, OUT, QKV, NARROW)
        + [(NARROW, f32), (NARROW, f32), (NARROW, bf16)],
        7,
        28,
        60.0,
    )
    lon_other = from_other_core(lon_other)
    pack = swap(pack, LON)
    (both,) = call(
        join_cores, [(lon_mine, VMEM), (lon_other, VMEM)], [(SUMS, bf16, VMEM)], [], 0, 12, 0.1
    )
    unpacked = pack.reshape(4, 4, 2 * NEAR, WIDTH).astype(f32)
    lon = call(
        sum_row,
        [(swap(both, CHIPS), VMEM)],
        [((12, WIDTH), f32, pl.ANY), ((4, WIDTH), f32, pl.ANY)],
        [],
        0,
        12,
        60.0,
    )
    parts = call(
        pick_y,
        [(core, SMEM), (column.reshape(4, 192, WIDTH), VMEM)],
        [((192, WIDTH), bf16, VMEM)] * 4,
        [],
        0,
        8,
        0.01,
    )
    parts = call(
        sum_pick_z,
        [(core, SMEM)] + [(part, VMEM) for part in trade(parts, "y")],
        [((48, WIDTH), bf16, VMEM)] * 4,
        low((4, 48, WIDTH)),
        0,
        8,
        0.01,
    )
    column = call(
        sum_column,
        [(part, VMEM) for part in trade(parts, ("h", "l"))],
        [((rows, lanes), f32, pl.ANY) for rows, lanes in ((12, WIDTH), (4, WIDTH), (16, WIDTH), (4, FF))],
        [],
        0,
        4,
        0.1,
    )
    return (
        unpacked[:, :, NEAR:],
        unpacked[:, :, :NEAR],
        *(array.T for array in lon),
        *(array.T for array in column),
    )


def solution(mesh):
    fine = Mesh(mesh.devices.reshape(4, 2, 4, 2, 2), ("x", "h", "y", "l", "c"))
    grid = P(("x", "h"), None, ("y", "l", "c"), None)
    columns = P(None, ("x", "h", "y", "l", "c"))
    return jax.shard_map(
        per_device,
        mesh=fine,
        in_specs=(grid, grid) + (P(),) * 6,
        out_specs=(grid, grid) + (columns,) * 6,
        check_vma=False,
    )
```

```python
import jax
import jax.numpy as jnp
from jax import lax
from jax.experimental import pallas as pl
from jax.experimental.pallas import tpu as pltpu
from jax.sharding import Mesh, PartitionSpec as P

HEADS = 8
WIDTH = 512
FF = 2048
HEAD = WIDTH // HEADS
SCALE = HEAD**-0.5
EPSILON = 1e-05
ROWS = 352
LATS = 32
NEAR = 22
PART = 11
PIECE = 13
LON = ("y", "l", "c")
TURN = ("h", "x", "y")
CHIPS = ("x", "h", "y", "l")
UNROLL = HEADS // 2
BLOCKS = ((0, 128), (128, 128), (256, 96))
f32 = jnp.float32
bf16 = jnp.bfloat16


def normalize(values):
    center = values - jnp.mean(values, axis=-1, keepdims=True)
    inverse = lax.rsqrt(jnp.mean(center * center, axis=-1, keepdims=True) + EPSILON)
    return center * inverse, inverse


def norm_back(scaled, inverse, upstream):
    return inverse * (
        upstream
        - jnp.mean(upstream, axis=-1, keepdims=True)
        - scaled * jnp.mean(upstream * scaled, axis=-1, keepdims=True)
    )


def dot(left, right, left_dim=1, right_dim=0):
    dims = (((left_dim,), (right_dim,)), ((), ()))
    return lax.dot_general(left, right, dims, preferred_element_type=f32)


def half_of(values, half):
    lanes = lax.broadcasted_iota(jnp.int32, values.shape, 1) // HEAD
    return jnp.where(lanes == half, values, jnp.zeros_like(values))


def pair_columns(part, pair):
    return pl.ds(pl.multiple_of(part * WIDTH + pair * 2 * HEAD, 2 * HEAD), 2 * HEAD)


def over_pairs(body):
    lax.fori_loop(0, HEADS // 2, lambda pair, _: body(pair) or 0, 0, unroll=UNROLL)


def row_probabilities(packed, pair, half):
    keys = half_of(packed[:, pair_columns(1, pair)] * SCALE, half)
    scores = dot(keys, packed[:, pair_columns(0, pair)], 1, 1)
    powers = jnp.exp(scores - jnp.max(scores, axis=0, keepdims=True))
    return (powers * (1.0 / jnp.sum(powers, axis=0, keepdims=True))).astype(bf16)


def put_mixed(turned, pair, half, rows, mixed):
    place = pl.ds(pl.multiple_of(pair * 2 * HEAD + half * HEAD, HEAD), HEAD)
    turned[place, rows] = mixed[half * HEAD : (half + 1) * HEAD]


def put_grads(grads, pair, rows, found):
    for part in range(3):
        both = half_of(found[0][part], 0) + half_of(found[1][part], 1)
        grads[rows, pair_columns(part, pair)] = both.astype(bf16)


def attend_rows(packed, turned):
    def one_pair(pair):
        values = packed[:, pair_columns(2, pair)]
        probs = [row_probabilities(packed, pair, half) for half in range(2)]
        for half in range(2):
            put_mixed(turned, pair, half, pl.ds(0, ROWS), dot(values, probs[half], 0, 0))

    over_pairs(one_pair)


def row_weights(packed_far, after, weights_far, packed, weights, semaphores):
    mover = Mover(semaphores)
    del after
    mover.start(packed_far, packed).wait()

    def one_pair(pair):
        for half in range(2):
            weights[pair * 2 + half] = row_probabilities(packed, pair, half)

    over_pairs(one_pair)
    mover.start(weights, weights_far).wait()


def attend_rows_back(packed, upstream, weights, grads):
    def one_pair(pair):
        queries, keys, values = (packed[:, pair_columns(p, pair)] for p in range(3))
        grad_mix = upstream[:, pair_columns(0, pair)]
        found = []
        for half in range(2):
            low = weights[pair * 2 + half]
            probs = low.astype(f32)
            grad_probs = dot(half_of(values, half), grad_mix, 1, 1)
            inner = jnp.sum(grad_probs * probs, axis=0, keepdims=True)
            grad_scores = (probs * (grad_probs - inner) * SCALE).astype(bf16)
            found.append(
                (dot(grad_scores, keys, 0, 0), dot(grad_scores, queries), dot(low, grad_mix))
            )
        put_grads(grads, pair, pl.ds(0, ROWS), found)

    over_pairs(one_pair)


def column_lanes(count):
    return lax.broadcasted_iota(jnp.int32, (LATS, count), 1) // LATS


def own_columns(square):
    count = square.shape[0]
    lanes = column_lanes(count)
    kept = square[:LATS]
    for column in range(1, count // LATS):
        kept = jnp.where(lanes == column, square[column * LATS : (column + 1) * LATS], kept)
    return kept


def to_square(kept):
    count = kept.shape[1]
    lanes = column_lanes(count)
    parts = [jnp.where(lanes == column, kept, 0.0) for column in range(count // LATS)]
    return jnp.concatenate(parts, axis=0).astype(bf16)


def attend_columns(packed, turned, probs):
    def scores(pair):
        for first, count in BLOCKS:
            rows = pl.ds(first, count)
            queries, keys = (packed[rows, pair_columns(p, pair)] for p in range(2))
            for half in range(2):
                square = dot(half_of(keys * SCALE, half), queries, 1, 1)
                probs[pair * 2 + half, :, rows] = own_columns(square)

    over_pairs(scores)
    powers = probs[...]
    powers = jnp.exp(powers - jnp.max(powers, axis=1, keepdims=True))
    probs[...] = powers * (1.0 / jnp.sum(powers, axis=1, keepdims=True))

    def mix(pair):
        for first, count in BLOCKS:
            rows = pl.ds(first, count)
            values = packed[rows, pair_columns(2, pair)]
            for half in range(2):
                square = to_square(probs[pair * 2 + half, :, rows])
                put_mixed(turned, pair, half, rows, dot(values, square, 0, 0))

    over_pairs(mix)


def attend_columns_back(packed, upstream, probs, grad_scores, grads):
    def products(pair):
        for first, count in BLOCKS:
            rows = pl.ds(first, count)
            values, grad_mix = packed[rows, pair_columns(2, pair)], upstream[rows, pair_columns(0, pair)]
            for half in range(2):
                square = dot(half_of(values, half), grad_mix, 1, 1)
                grad_scores[pair * 2 + half, :, rows] = own_columns(square)

    over_pairs(products)
    grad_probs = grad_scores[...]
    inner = jnp.sum(grad_probs * probs[...], axis=1, keepdims=True)
    grad_scores[...] = probs[...] * (grad_probs - inner) * SCALE

    def combine(pair):
        for first, count in BLOCKS:
            rows = pl.ds(first, count)
            queries, keys = (packed[rows, pair_columns(p, pair)] for p in range(2))
            grad_mix = upstream[rows, pair_columns(0, pair)]
            found = []
            for half in range(2):
                square = to_square(grad_scores[pair * 2 + half, :, rows])
                weights = to_square(probs[pair * 2 + half, :, rows])
                found.append(
                    (dot(square, keys, 0, 0), dot(square, queries), dot(weights, grad_mix))
                )
            put_grads(grads, pair, rows, found)

    over_pairs(combine)


def project(normed, inproj, packed):
    for part in range(3):
        columns = pl.ds(part * WIDTH, WIDTH)
        packed[:, columns] = dot(normed, inproj[:, columns]).astype(bf16)


class Mover:
    def __init__(self, semaphores):
        self.semaphores, self.count = semaphores, 0

    def start(self, source, target):
        copy = pltpu.make_async_copy(source, target, self.semaphores.at[self.count])
        self.count += 1
        copy.start()
        return copy


def row_forward(
    pack, inproj_far, outproj_far,
    out, tokens_far, normed_far, packed_far, mixed_far,
    inproj, outproj, tokens, normed, packed, mixed, hidden, cotangent, turned, semaphores,
):
    mover = Mover(semaphores)
    inproj_in = mover.start(inproj_far, inproj)
    outproj_in = mover.start(outproj_far, outproj)
    for block in range(16):
        piece = pack[block].astype(f32)
        rows = pl.ds(block * NEAR, NEAR)
        hidden[rows, :] = piece[:NEAR]
        cotangent[rows, :] = piece[NEAR:]
    values = hidden[...]
    tokens[...] = values.astype(bf16)
    normed[...] = normalize(values)[0].astype(bf16)
    leaving = [mover.start(tokens, tokens_far), mover.start(normed, normed_far)]
    inproj_in.wait()
    project(normed[...], inproj, packed)
    leaving.append(mover.start(packed, packed_far))
    attend_rows(packed, turned)
    mixed[...] = turned[...].T.astype(bf16)
    leaving.append(mover.start(mixed, mixed_far))
    outproj_in.wait()
    hidden[...] += dot(mixed[...], outproj[...])
    for block in range(LATS):
        rows = pl.ds(block * PART, PART)
        out[block] = jnp.concatenate([hidden[rows, :], cotangent[rows, :]], axis=0).astype(bf16)
    for copy in leaving:
        copy.wait()


def row_backward(
    pack, tokens_far, packed_far, weights_far, inproj_far, outproj_far,
    out, grads_far, low_far,
    tokens, packed, weights, inproj, outproj, grads, low, hidden, output, upstream, semaphores,
):
    mover = Mover(semaphores)
    outproj_in = mover.start(outproj_far, outproj)
    coming = [mover.start(packed_far, packed), mover.start(weights_far, weights)]
    inproj_in = mover.start(inproj_far, inproj)
    tokens_in = mover.start(tokens_far, tokens)
    for block in range(LATS):
        piece = pack[block].astype(f32)
        rows = pl.ds(block * PART, PART)
        hidden[rows, :] = piece[:PART]
        output[rows, :] = piece[PART:]
    low[...] = hidden[...].astype(bf16)
    leaving = [mover.start(low, low_far)]
    outproj_in.wait()
    upstream[...] = dot(low[...], outproj[...], 1, 1).astype(bf16)
    for copy in coming:
        copy.wait()
    attend_rows_back(packed, upstream, weights, grads)
    leaving.append(mover.start(grads, grads_far))
    inproj_in.wait()
    grad_normed = dot(grads[...], inproj[...], 1, 1)
    tokens_in.wait()
    hidden[...] += norm_back(*normalize(tokens[...].astype(f32)), grad_normed)
    for block in range(16):
        rows = pl.ds(block * NEAR, NEAR)
        out[block] = jnp.concatenate([hidden[rows, :], output[rows, :]], axis=0).astype(bf16)
    for copy in leaving:
        copy.wait()


def to_columns(pack, columns):
    for lat in range(LATS):
        piece = pack[lat].astype(f32)
        for tile in range(4):
            lanes = slice(tile * 128, (tile + 1) * 128)
            columns[tile, pl.ds(lat, 2 * PART, stride=LATS), :] = piece[:, lanes]


def joined(columns, unit):
    rows = pl.ds(unit * ROWS, ROWS)
    return jnp.concatenate([columns[tile, rows, :] for tile in range(4)], axis=1)


def put_columns(columns, unit, values):
    for tile in range(4):
        columns[tile, pl.ds(unit * ROWS, ROWS), :] = values[:, tile * 128 : (tile + 1) * 128]


def from_columns(out, columns):
    for lat in range(LATS):
        rows = pl.ds(lat, 2 * PART, stride=LATS)
        piece = jnp.concatenate([columns[tile, rows, :] for tile in range(4)], axis=1)
        out[lat] = piece.astype(bf16)


def column_both(
    pack, inproj_far, outproj_far, mlp_in_far, mlp_out_far,
    out, normed_far, mixed_far, grads_far, low_far, normed_mlp_far, activated_far, grad_inner_far, cotangent_far,
    inproj, outproj, mlp_in, mlp_out, normed, mixed, grads, low, normed_mlp, activated, grad_inner, cotangent,
    packed, upstream, columns, turned, hidden_one, hidden, grad_normed, output, probs, grad_scores,
    semaphores,
):
    mover = Mover(semaphores)
    inproj_in = mover.start(inproj_far, inproj)
    outproj_in = mover.start(outproj_far, outproj)
    coming = [mover.start(mlp_in_far, mlp_in), mover.start(mlp_out_far, mlp_out)]
    to_columns(pack, columns)
    hidden_one[...] = joined(columns, 0)
    cotangent[...] = joined(columns, 1).astype(bf16)
    normed[...] = normalize(hidden_one[...])[0].astype(bf16)
    leaving = [mover.start(cotangent, cotangent_far), mover.start(normed, normed_far)]
    inproj_in.wait()
    project(normed[...], inproj, packed)
    attend_columns(packed, turned, probs)
    mixed[...] = turned[...].T.astype(bf16)
    leaving.append(mover.start(mixed, mixed_far))
    outproj_in.wait()
    hidden[...] = hidden_one[...] + dot(mixed[...], outproj[...])
    normed_mlp[...] = normalize(hidden[...])[0].astype(bf16)
    leaving.append(mover.start(normed_mlp, normed_mlp_far))
    output[...] = hidden[...]
    grad_normed[...] = jnp.zeros_like(grad_normed)
    for copy in coming:
        copy.wait()

    def one_chunk(chunk, _):
        chosen = pl.ds(pl.multiple_of(chunk * 512, 512), 512)
        inner = dot(normed_mlp[...], mlp_in[:, chosen])
        spread = 0.5 * (1.0 + lax.erf(inner * 2.0**-0.5))
        slope = spread + inner * (0.5 / jnp.pi) ** 0.5 * jnp.exp(-0.5 * inner * inner)
        active = (inner * spread).astype(bf16)
        activated[:, chosen] = active
        output[...] += dot(active, mlp_out[chosen, :])
        grad = (dot(cotangent[...], mlp_out[chosen, :], 1, 1) * slope).astype(bf16)
        grad_inner[:, chosen] = grad
        grad_normed[...] += dot(grad, mlp_in[:, chosen], 1, 1)
        return 0

    lax.fori_loop(0, FF // 512, one_chunk, 0, unroll=4)
    leaving.append(mover.start(activated, activated_far))
    leaving.append(mover.start(grad_inner, grad_inner_far))
    put_columns(columns, 1, output[...])
    back = norm_back(*normalize(hidden[...]), grad_normed[...])
    hidden[...] = cotangent[...].astype(f32) + back
    low[...] = hidden[...].astype(bf16)
    leaving.append(mover.start(low, low_far))
    upstream[...] = dot(low[...], outproj[...], 1, 1).astype(bf16)
    attend_columns_back(packed, upstream, probs, grad_scores, grads)
    leaving.append(mover.start(grads, grads_far))
    back = norm_back(*normalize(hidden_one[...]), dot(grads[...], inproj[...], 1, 1))
    put_columns(columns, 0, hidden[...] + back)
    from_columns(out, columns)
    for copy in leaving:
        copy.wait()


def block_terms(block, grads, normed, low, mixed):
    wide = dot(grads[:, block * 384 : (block + 1) * 384], normed[...], 0, 0)
    slim = dot(low[:, block * 128 : (block + 1) * 128], mixed[...], 0, 0)
    return [wide.reshape(32, 12, WIDTH), slim.reshape(32, 4, WIDTH)]


def put_terms(place, terms, block, rows, mine, others):
    both = jnp.concatenate(terms, axis=1).astype(bf16)
    both = both.reshape(2, 4, 2, 2, both.shape[1], WIDTH)
    for high in range(2):
        even, odd = both[high, :, :, 0], both[high, :, :, 1]
        mine[block, :, high, :, rows, :] = jnp.where(place[0] == 0, even, odd)
        leaving = jnp.where(place[0] == 0, odd, even)
        for row in range(4):
            for low_z in range(2):
                piece, chip = divmod(16 * block + 4 * row + 2 * high + low_z, PIECE)
                others[piece][chip, rows, :] = leaving[row, low_z]


def column_terms(place, *refs):
    far, mine, others, near, semaphores = refs[:8], refs[8], refs[9:14], refs[14:22], refs[22]
    mover = Mover(semaphores)
    coming = [mover.start(source, target) for source, target in zip(far, near)]
    grads, normed, low, mixed, normed_mlp, grad_inner, activated, cotangent = near
    for copy in coming[:4]:
        copy.wait()
    for block in range(4):
        terms = block_terms(block, grads, normed, low, mixed)
        put_terms(place, terms, block, pl.ds(0, 16), mine, others)
    for copy in coming[4:]:
        copy.wait()
    for block in range(4):
        inner = dot(grad_inner[:, block * 512 : (block + 1) * 512], normed_mlp[...], 0, 0)
        outer = dot(cotangent[:, block * 128 : (block + 1) * 128], activated[...], 0, 0)
        terms = [inner.reshape(32, 16, WIDTH)]
        for part in range(4):
            terms.append(outer[:, part * WIDTH : (part + 1) * WIDTH].reshape(32, 4, WIDTH))
        put_terms(place, terms, block, pl.ds(16, 32), mine, others)


def row_terms(place, *refs):
    far, mine, others, near, semaphores = refs[:4], refs[4], refs[5:7], refs[7:11], refs[11]
    mover = Mover(semaphores)
    for copy in [mover.start(source, target) for source, target in zip(far, near)]:
        copy.wait()
    for block in range(4):
        terms = jnp.concatenate(block_terms(block, *near), axis=1)
        terms = terms.astype(bf16).reshape(16, 2, 16, WIDTH)
        mine[pl.ds(block * 16, 16)] = jnp.where(place[0] == 0, terms[:, 0], terms[:, 1])
        leaving = jnp.where(place[0] == 0, terms[:, 1], terms[:, 0])
        others[block // 2][pl.ds(block % 2 * 16, 16)] = leaving


def join_cores(mine, first, second, out):
    for block in range(4):
        chips = pl.ds(block * 16, 16)
        other = (first, second)[block // 2][pl.ds(block % 2 * 16, 16)]
        out[chips] = (mine[chips].astype(f32) + other.astype(f32)).astype(bf16)


def add_cores(mine, *refs):
    others, out_far, total, semaphores = refs[:5], *refs[5:]
    mover = Mover(semaphores)
    leaving = []
    for block in range(4):
        for place in range(16):
            row, rest = divmod(place, 4)
            high, low_z = divmod(rest, 2)
            piece, chip = divmod(16 * block + place, PIECE)
            own = mine[block, row, high, low_z].astype(f32)
            total[block, row, high, low_z] = (own + others[piece][chip].astype(f32)).astype(bf16)
        leaving.append(mover.start(total.at[block], out_far.at[block]))
    for copy in leaving:
        copy.wait()


def sum_row(parts, lon_in, lon_out):
    total = jnp.sum(parts[...].astype(f32), axis=0)
    lon_in[...] = total[0:12]
    lon_out[...] = total[12:16]


def pick_y(place, blocks, *outs):
    for step in range(4):
        outs[step][...] = blocks[jnp.bitwise_xor(place[1], step)]


def sum_pick_z(place, *refs):
    parts, outs, total = refs[:4], refs[4:8], refs[8]
    added = sum(part[...].astype(f32) for part in parts)
    total[...] = added.astype(bf16).reshape(total.shape)
    for step in range(4):
        outs[step][...] = total[jnp.bitwise_xor(place[2], step)]


def sum_column(*refs):
    parts, (lat_in, lat_out, wide_in, wide_out) = refs[:4], refs[4:]
    total = sum(part[...].astype(f32) for part in parts)
    lat_in[...] = total[0:12]
    lat_out[...] = total[12:16]
    wide_in[...] = total[16:32]
    for part in range(4):
        wide_out[:, part * WIDTH : (part + 1) * WIDTH] = total[32 + 4 * part : 36 + 4 * part]


SMEM, VMEM, HBM = pltpu.SMEM, pltpu.VMEM, pltpu.HBM


def call(kernel, args, outs, scratch, semaphores, megabytes, gigaflops, aliases=None):
    arrays = [
        pltpu.with_memory_space_constraint(array, HBM) if place is HBM else array
        for array, place in args
    ]
    scratch = [pltpu.VMEM(shape, kind) for shape, kind in scratch]
    if semaphores:
        scratch.append(pltpu.SemaphoreType.DMA((semaphores,)))
    return pl.pallas_call(
        kernel,
        out_shape=[
            jax.ShapeDtypeStruct(shape, kind) if place is pl.ANY else place(shape, kind)
            for shape, kind, place in outs
        ],
        in_specs=[pl.BlockSpec(memory_space=place) for _, place in args],
        out_specs=[
            pl.BlockSpec(memory_space=VMEM if place is pl.ANY else place) for _, _, place in outs
        ],
        scratch_shapes=scratch,
        compiler_params=pltpu.CompilerParams(vmem_limit_bytes=megabytes << 20),
        cost_estimate=pl.CostEstimate(
            flops=int(gigaflops * 1e9), bytes_accessed=1 << 16, transcendentals=0
        ),
        input_output_aliases=aliases or {},
    )(*arrays)


def swap(array, axes):
    return lax.all_to_all(array, axes, split_axis=0, concat_axis=0, tiled=True)


def trade(parts, axes):
    moved = [
        lax.ppermute(part, axes, [(place, place ^ step) for place in range(4)])
        for step, part in enumerate(parts)
        if step
    ]
    return [parts[0], *moved]


def from_other_core(array):
    return lax.ppermute(array, "c", [(0, 1), (1, 0)])


NARROW = (ROWS, WIDTH)
QKV = (ROWS, 3 * WIDTH)
WIDE = (ROWS, FF)
TILES = (4, 2 * ROWS, 128)
TURNED = (WIDTH, ROWS)
TO_TURN = (LATS, 2 * PART, WIDTH)
TO_LON = (16, 2 * NEAR, WIDTH)
LON_WEIGHTS = (HEADS, ROWS, ROWS)
LAT_PROBS = (HEADS, LATS, ROWS)
IN, OUT, MLP_IN, MLP_OUT = (WIDTH, 3 * WIDTH), (WIDTH, WIDTH), (WIDTH, FF), (FF, WIDTH)
SUMS = (64, 16, WIDTH)
BY_CHIP = (4, 4, 2, 2, 48, WIDTH)


def low(*shapes):
    return [(shape, bf16) for shape in shapes]


def far(*shapes):
    return [(shape, bf16, HBM) for shape in shapes]


def all_far(*arrays):
    return [(array, HBM) for array in arrays]


def per_device(tokens, cotangent, inproj_lon, outproj_lon, inproj_lat, outproj_lat, mlp_in, mlp_out):
    core = jnp.stack([lax.axis_index(axes) for axes in ("c", "y", ("h", "l"))]).astype(jnp.int32)
    pack = jnp.concatenate([tokens, cotangent], axis=2).reshape(TO_LON)
    pack, row_tokens, row_normed, row_packed, row_mixed = call(
        row_forward,
        [(swap(pack, LON), VMEM)] + all_far(inproj_lon, outproj_lon),
        [(TO_TURN, bf16, VMEM)] + far(NARROW, NARROW, QKV, NARROW),
        low(IN, OUT, NARROW, NARROW, QKV, NARROW) + [(NARROW, f32), (NARROW, f32), (TURNED, f32)],
        6,
        20,
        5.0,
    )
    pack, normed, mixed, grads, upstream, *saved = call(
        column_both,
        [(swap(pack, TURN), VMEM)] + all_far(inproj_lat, outproj_lat, mlp_in, mlp_out),
        [(TO_TURN, bf16, VMEM)] + far(NARROW, NARROW, QKV, NARROW, NARROW, WIDE, WIDE, NARROW),
        low(IN, OUT, MLP_IN, MLP_OUT, NARROW, NARROW, QKV, NARROW, NARROW, WIDE, WIDE, NARROW, QKV, NARROW)
        + [(TILES, f32), (TURNED, f32)] + [(NARROW, f32)] * 4 + [(LAT_PROBS, f32)] * 2,
        12,
        36,
        20.0,
    )
    mine, *others = call(
        column_terms,
        [(core, SMEM)] + all_far(grads, normed, upstream, mixed, *(saved[i] for i in (0, 2, 1, 3))),
        [(BY_CHIP, bf16, VMEM)] + [((PIECE, 48, WIDTH), bf16, VMEM)] * 5,
        low(QKV, NARROW, NARROW, NARROW, NARROW, WIDE, WIDE, NARROW),
        8,
        32,
        0.1,
    )
    (weights,) = call(
        row_weights,
        [(row_packed, HBM), (mine, pl.ANY)],
        far(LON_WEIGHTS),
        low(QKV, LON_WEIGHTS),
        2,
        12,
        0.1,
    )
    (column,) = call(
        add_cores,
        [(mine, VMEM)] + [(from_other_core(other), VMEM) for other in others],
        far(BY_CHIP),
        low(BY_CHIP),
        4,
        20,
        0.1,
    )
    column = lax.psum_scatter(column.reshape(3072, WIDTH), "x", scatter_dimension=0, tiled=True)
    pack, grads, upstream = call(
        row_backward,
        [(swap(pack, TURN), VMEM)]
        + all_far(row_tokens, row_packed, weights, inproj_lon, outproj_lon),
        [(TO_LON, bf16, pl.ANY)] + far(QKV, NARROW),
        low(NARROW, QKV, LON_WEIGHTS, IN, OUT, QKV, NARROW)
        + [(NARROW, f32), (NARROW, f32), (NARROW, bf16)],
        7,
        28,
        60.0,
    )
    lon_mine, *lon_others = call(
        row_terms,
        [(core, SMEM)] + all_far(grads, row_normed, upstream, row_mixed),
        [(SUMS, bf16, VMEM)] + [((32, 16, WIDTH), bf16, VMEM)] * 2,
        low(QKV, NARROW, NARROW, NARROW),
        4,
        20,
        0.1,
    )
    pack = swap(pack, LON)
    (both,) = call(
        join_cores, [(lon_mine, VMEM)] + [(from_other_core(other), VMEM) for other in lon_others], [(SUMS, bf16, VMEM)], [], 0, 12, 0.1
    )
    unpacked = pack.reshape(4, 4, 2 * NEAR, WIDTH).astype(f32)
    lon = call(
        sum_row,
        [(swap(both, CHIPS), VMEM)],
        [((12, WIDTH), f32, pl.ANY), ((4, WIDTH), f32, pl.ANY)],
        [],
        0,
        12,
        60.0,
    )
    parts = call(
        pick_y,
        [(core, SMEM), (column.reshape(4, 192, WIDTH), VMEM)],
        [((192, WIDTH), bf16, VMEM)] * 4,
        [],
        0,
        8,
        0.01,
    )
    parts = call(
        sum_pick_z,
        [(core, SMEM)] + [(part, VMEM) for part in trade(parts, "y")],
        [((48, WIDTH), bf16, VMEM)] * 4,
        low((4, 48, WIDTH)),
        0,
        8,
        0.01,
    )
    column = call(
        sum_column,
        [(part, VMEM) for part in trade(parts, ("h", "l"))],
        [((rows, lanes), f32, pl.ANY) for rows, lanes in ((12, WIDTH), (4, WIDTH), (16, WIDTH), (4, FF))],
        [],
        0,
        4,
        0.1,
    )
    return (
        unpacked[:, :, NEAR:],
        unpacked[:, :, :NEAR],
        *(array.T for array in lon),
        *(array.T for array in column),
    )


def solution(mesh):
    fine = Mesh(mesh.devices.reshape(4, 2, 4, 2, 2), ("x", "h", "y", "l", "c"))
    grid = P(("x", "h"), None, ("y", "l", "c"), None)
    columns = P(None, ("x", "h", "y", "l", "c"))
    return jax.shard_map(
        per_device,
        mesh=fine,
        in_specs=(grid, grid) + (P(),) * 6,
        out_specs=(grid, grid) + (columns,) * 6,
        check_vma=False,
    )
```

```python
import jax
import jax.numpy as jnp
from jax import lax
from jax.experimental import pallas as pl
from jax.experimental.pallas import tpu as pltpu
from jax.sharding import Mesh, PartitionSpec as P

HEADS = 8
WIDTH = 512
FF = 2048
HEAD = WIDTH // HEADS
SCALE = HEAD**-0.5
EPSILON = 1e-05
ROWS = 352
LATS = 32
NEAR = 22
PART = 11
PIECE = 13
LON = ("y", "l", "c")
TURN = ("h", "x", "y")
CHIPS = ("x", "h", "y", "l")
UNROLL = HEADS // 2
BLOCKS = ((0, 128), (128, 128), (256, 96))
f32 = jnp.float32
bf16 = jnp.bfloat16


def normalize(values):
    center = values - jnp.mean(values, axis=-1, keepdims=True)
    inverse = lax.rsqrt(jnp.mean(center * center, axis=-1, keepdims=True) + EPSILON)
    return center * inverse, inverse


def norm_back(scaled, inverse, upstream):
    return inverse * (
        upstream
        - jnp.mean(upstream, axis=-1, keepdims=True)
        - scaled * jnp.mean(upstream * scaled, axis=-1, keepdims=True)
    )


def dot(left, right, left_dim=1, right_dim=0):
    dims = (((left_dim,), (right_dim,)), ((), ()))
    return lax.dot_general(left, right, dims, preferred_element_type=f32)


def half_of(values, half):
    lanes = lax.broadcasted_iota(jnp.int32, values.shape, 1) // HEAD
    return jnp.where(lanes == half, values, jnp.zeros_like(values))


def pair_columns(part, pair):
    return pl.ds(pl.multiple_of(part * WIDTH + pair * 2 * HEAD, 2 * HEAD), 2 * HEAD)


def over_pairs(body):
    lax.fori_loop(0, HEADS // 2, lambda pair, _: body(pair) or 0, 0, unroll=UNROLL)


def row_probabilities(packed, pair, half):
    keys = half_of(packed[:, pair_columns(1, pair)] * SCALE, half)
    scores = dot(keys, packed[:, pair_columns(0, pair)], 1, 1)
    powers = jnp.exp(scores - jnp.max(scores, axis=0, keepdims=True))
    return (powers * (1.0 / jnp.sum(powers, axis=0, keepdims=True))).astype(bf16)


def put_mixed(turned, pair, half, rows, mixed):
    place = pl.ds(pl.multiple_of(pair * 2 * HEAD + half * HEAD, HEAD), HEAD)
    turned[place, rows] = mixed[half * HEAD : (half + 1) * HEAD]


def put_grads(grads, pair, rows, found):
    for part in range(3):
        both = half_of(found[0][part], 0) + half_of(found[1][part], 1)
        grads[rows, pair_columns(part, pair)] = both.astype(bf16)


def attend_rows(packed, turned):
    def one_pair(pair):
        values = packed[:, pair_columns(2, pair)]
        probs = [row_probabilities(packed, pair, half) for half in range(2)]
        for half in range(2):
            put_mixed(turned, pair, half, pl.ds(0, ROWS), dot(values, probs[half], 0, 0))

    over_pairs(one_pair)


def row_weights(packed_far, after, weights_far, packed, weights, semaphores):
    mover = Mover(semaphores)
    del after
    mover.start(packed_far, packed).wait()

    def one_pair(pair):
        for half in range(2):
            weights[pair * 2 + half] = row_probabilities(packed, pair, half)

    over_pairs(one_pair)
    mover.start(weights, weights_far).wait()


def attend_rows_back(packed, upstream, weights, grads):
    def one_pair(pair):
        queries, keys, values = (packed[:, pair_columns(p, pair)] for p in range(3))
        grad_mix = upstream[:, pair_columns(0, pair)]
        found = []
        for half in range(2):
            low = weights[pair * 2 + half]
            probs = low.astype(f32)
            grad_probs = dot(half_of(values, half), grad_mix, 1, 1)
            inner = jnp.sum(grad_probs * probs, axis=0, keepdims=True)
            grad_scores = (probs * (grad_probs - inner) * SCALE).astype(bf16)
            found.append(
                (dot(grad_scores, keys, 0, 0), dot(grad_scores, queries), dot(low, grad_mix))
            )
        put_grads(grads, pair, pl.ds(0, ROWS), found)

    over_pairs(one_pair)


def column_lanes(count):
    return lax.broadcasted_iota(jnp.int32, (LATS, count), 1) // LATS


def own_columns(square):
    count = square.shape[0]
    lanes = column_lanes(count)
    kept = square[:LATS]
    for column in range(1, count // LATS):
        kept = jnp.where(lanes == column, square[column * LATS : (column + 1) * LATS], kept)
    return kept


def to_square(kept):
    count = kept.shape[1]
    lanes = column_lanes(count)
    parts = [jnp.where(lanes == column, kept, 0.0) for column in range(count // LATS)]
    return jnp.concatenate(parts, axis=0).astype(bf16)


def attend_columns(packed, turned, probs):
    def scores(pair):
        for first, count in BLOCKS:
            rows = pl.ds(first, count)
            queries, keys = (packed[rows, pair_columns(p, pair)] for p in range(2))
            for half in range(2):
                square = dot(half_of(keys * SCALE, half), queries, 1, 1)
                probs[pair * 2 + half, :, rows] = own_columns(square)

    over_pairs(scores)
    powers = probs[...]
    powers = jnp.exp(powers - jnp.max(powers, axis=1, keepdims=True))
    probs[...] = powers * (1.0 / jnp.sum(powers, axis=1, keepdims=True))

    def mix(pair):
        for first, count in BLOCKS:
            rows = pl.ds(first, count)
            values = packed[rows, pair_columns(2, pair)]
            for half in range(2):
                square = to_square(probs[pair * 2 + half, :, rows])
                put_mixed(turned, pair, half, rows, dot(values, square, 0, 0))

    over_pairs(mix)


def attend_columns_back(packed, upstream, probs, grad_scores, grads):
    def products(pair):
        for first, count in BLOCKS:
            rows = pl.ds(first, count)
            values, grad_mix = packed[rows, pair_columns(2, pair)], upstream[rows, pair_columns(0, pair)]
            for half in range(2):
                square = dot(half_of(values, half), grad_mix, 1, 1)
                grad_scores[pair * 2 + half, :, rows] = own_columns(square)

    over_pairs(products)
    grad_probs = grad_scores[...]
    inner = jnp.sum(grad_probs * probs[...], axis=1, keepdims=True)
    grad_scores[...] = probs[...] * (grad_probs - inner) * SCALE

    def combine(pair):
        for first, count in BLOCKS:
            rows = pl.ds(first, count)
            queries, keys = (packed[rows, pair_columns(p, pair)] for p in range(2))
            grad_mix = upstream[rows, pair_columns(0, pair)]
            found = []
            for half in range(2):
                square = to_square(grad_scores[pair * 2 + half, :, rows])
                weights = to_square(probs[pair * 2 + half, :, rows])
                found.append(
                    (dot(square, keys, 0, 0), dot(square, queries), dot(weights, grad_mix))
                )
            put_grads(grads, pair, rows, found)

    over_pairs(combine)


def project(normed, inproj, packed):
    for part in range(3):
        columns = pl.ds(part * WIDTH, WIDTH)
        packed[:, columns] = dot(normed, inproj[:, columns]).astype(bf16)


class Mover:
    def __init__(self, semaphores):
        self.semaphores, self.count = semaphores, 0

    def start(self, source, target):
        copy = pltpu.make_async_copy(source, target, self.semaphores.at[self.count])
        self.count += 1
        copy.start()
        return copy


def row_forward(
    pack, inproj_far, outproj_far,
    out, tokens_far, normed_far, packed_far, mixed_far,
    inproj, outproj, tokens, normed, packed, mixed, hidden, cotangent, turned, semaphores,
):
    mover = Mover(semaphores)
    inproj_in = mover.start(inproj_far, inproj)
    outproj_in = mover.start(outproj_far, outproj)
    for block in range(16):
        piece = pack[block].astype(f32)
        rows = pl.ds(block * NEAR, NEAR)
        hidden[rows, :] = piece[:NEAR]
        cotangent[rows, :] = piece[NEAR:]
    values = hidden[...]
    tokens[...] = values.astype(bf16)
    normed[...] = normalize(values)[0].astype(bf16)
    leaving = [mover.start(tokens, tokens_far), mover.start(normed, normed_far)]
    inproj_in.wait()
    project(normed[...], inproj, packed)
    leaving.append(mover.start(packed, packed_far))
    attend_rows(packed, turned)
    mixed[...] = turned[...].T.astype(bf16)
    leaving.append(mover.start(mixed, mixed_far))
    outproj_in.wait()
    hidden[...] += dot(mixed[...], outproj[...])
    for block in range(LATS):
        rows = pl.ds(block * PART, PART)
        out[block] = jnp.concatenate([hidden[rows, :], cotangent[rows, :]], axis=0).astype(bf16)
    for copy in leaving:
        copy.wait()


def row_backward(
    pack, tokens_far, packed_far, weights_far, inproj_far, outproj_far,
    out, grads_far, low_far,
    tokens, packed, weights, inproj, outproj, grads, low, hidden, output, upstream, semaphores,
):
    mover = Mover(semaphores)
    outproj_in = mover.start(outproj_far, outproj)
    coming = [mover.start(packed_far, packed), mover.start(weights_far, weights)]
    inproj_in = mover.start(inproj_far, inproj)
    tokens_in = mover.start(tokens_far, tokens)
    for block in range(LATS):
        piece = pack[block].astype(f32)
        rows = pl.ds(block * PART, PART)
        hidden[rows, :] = piece[:PART]
        output[rows, :] = piece[PART:]
    low[...] = hidden[...].astype(bf16)
    leaving = [mover.start(low, low_far)]
    outproj_in.wait()
    upstream[...] = dot(low[...], outproj[...], 1, 1).astype(bf16)
    for copy in coming:
        copy.wait()
    attend_rows_back(packed, upstream, weights, grads)
    leaving.append(mover.start(grads, grads_far))
    inproj_in.wait()
    grad_normed = dot(grads[...], inproj[...], 1, 1)
    tokens_in.wait()
    hidden[...] += norm_back(*normalize(tokens[...].astype(f32)), grad_normed)
    for block in range(16):
        rows = pl.ds(block * NEAR, NEAR)
        out[block] = jnp.concatenate([hidden[rows, :], output[rows, :]], axis=0).astype(bf16)
    for copy in leaving:
        copy.wait()


def to_columns(pack, columns):
    for lat in range(LATS):
        piece = pack[lat].astype(f32)
        for tile in range(4):
            lanes = slice(tile * 128, (tile + 1) * 128)
            columns[tile, pl.ds(lat, 2 * PART, stride=LATS), :] = piece[:, lanes]


def joined(columns, unit):
    rows = pl.ds(unit * ROWS, ROWS)
    return jnp.concatenate([columns[tile, rows, :] for tile in range(4)], axis=1)


def put_columns(columns, unit, values):
    for tile in range(4):
        columns[tile, pl.ds(unit * ROWS, ROWS), :] = values[:, tile * 128 : (tile + 1) * 128]


def from_columns(out, columns):
    for lat in range(LATS):
        rows = pl.ds(lat, 2 * PART, stride=LATS)
        piece = jnp.concatenate([columns[tile, rows, :] for tile in range(4)], axis=1)
        out[lat] = piece.astype(bf16)


def column_both(
    pack, inproj_far, outproj_far, mlp_in_far, mlp_out_far,
    out, normed_far, mixed_far, grads_far, low_far, normed_mlp_far, activated_far, grad_inner_far, cotangent_far,
    inproj, outproj, mlp_in, mlp_out, normed, mixed, grads, low, normed_mlp, activated, grad_inner, cotangent,
    packed, upstream, columns, turned, hidden_one, hidden, grad_normed, output, probs, grad_scores,
    semaphores,
):
    mover = Mover(semaphores)
    inproj_in = mover.start(inproj_far, inproj)
    outproj_in = mover.start(outproj_far, outproj)
    coming = [mover.start(mlp_in_far, mlp_in), mover.start(mlp_out_far, mlp_out)]
    to_columns(pack, columns)
    hidden_one[...] = joined(columns, 0)
    cotangent[...] = joined(columns, 1).astype(bf16)
    normed[...] = normalize(hidden_one[...])[0].astype(bf16)
    leaving = [mover.start(cotangent, cotangent_far), mover.start(normed, normed_far)]
    inproj_in.wait()
    project(normed[...], inproj, packed)
    attend_columns(packed, turned, probs)
    mixed[...] = turned[...].T.astype(bf16)
    leaving.append(mover.start(mixed, mixed_far))
    outproj_in.wait()
    hidden[...] = hidden_one[...] + dot(mixed[...], outproj[...])
    normed_mlp[...] = normalize(hidden[...])[0].astype(bf16)
    leaving.append(mover.start(normed_mlp, normed_mlp_far))
    output[...] = hidden[...]
    grad_normed[...] = jnp.zeros_like(grad_normed)
    for copy in coming:
        copy.wait()

    def one_chunk(chunk, _):
        chosen = pl.ds(pl.multiple_of(chunk * 512, 512), 512)
        inner = dot(normed_mlp[...], mlp_in[:, chosen])
        spread = 0.5 * (1.0 + lax.erf(inner * 2.0**-0.5))
        slope = spread + inner * (0.5 / jnp.pi) ** 0.5 * jnp.exp(-0.5 * inner * inner)
        active = (inner * spread).astype(bf16)
        activated[:, chosen] = active
        output[...] += dot(active, mlp_out[chosen, :])
        grad = (dot(cotangent[...], mlp_out[chosen, :], 1, 1) * slope).astype(bf16)
        grad_inner[:, chosen] = grad
        grad_normed[...] += dot(grad, mlp_in[:, chosen], 1, 1)
        return 0

    lax.fori_loop(0, FF // 512, one_chunk, 0, unroll=4)
    leaving.append(mover.start(activated, activated_far))
    leaving.append(mover.start(grad_inner, grad_inner_far))
    put_columns(columns, 1, output[...])
    back = norm_back(*normalize(hidden[...]), grad_normed[...])
    hidden[...] = cotangent[...].astype(f32) + back
    low[...] = hidden[...].astype(bf16)
    leaving.append(mover.start(low, low_far))
    upstream[...] = dot(low[...], outproj[...], 1, 1).astype(bf16)
    attend_columns_back(packed, upstream, probs, grad_scores, grads)
    leaving.append(mover.start(grads, grads_far))
    back = norm_back(*normalize(hidden_one[...]), dot(grads[...], inproj[...], 1, 1))
    put_columns(columns, 0, hidden[...] + back)
    from_columns(out, columns)
    for copy in leaving:
        copy.wait()


def block_terms(block, grads, normed, low, mixed):
    wide = dot(grads[:, block * 384 : (block + 1) * 384], normed[...], 0, 0)
    slim = dot(low[:, block * 128 : (block + 1) * 128], mixed[...], 0, 0)
    return [wide.reshape(32, 12, WIDTH), slim.reshape(32, 4, WIDTH)]


def put_terms(place, terms, block, rows, mine, others):
    both = jnp.concatenate(terms, axis=1).astype(bf16)
    both = both.reshape(2, 4, 2, 2, both.shape[1], WIDTH)
    for high in range(2):
        even, odd = both[high, :, :, 0], both[high, :, :, 1]
        mine[block, :, high, :, rows, :] = jnp.where(place[0] == 0, even, odd)
        leaving = jnp.where(place[0] == 0, odd, even)
        for row in range(4):
            for low_z in range(2):
                piece, chip = divmod(16 * block + 4 * row + 2 * high + low_z, PIECE)
                others[piece][chip, rows, :] = leaving[row, low_z]


def column_terms(place, *refs):
    far, mine, others, near, semaphores = refs[:8], refs[8], refs[9:14], refs[14:22], refs[22]
    mover = Mover(semaphores)
    coming = [mover.start(source, target) for source, target in zip(far, near)]
    grads, normed, low, mixed, normed_mlp, grad_inner, activated, cotangent = near
    for copy in coming[:4]:
        copy.wait()
    for block in range(4):
        terms = block_terms(block, grads, normed, low, mixed)
        put_terms(place, terms, block, pl.ds(0, 16), mine, others)
    for copy in coming[4:]:
        copy.wait()
    for block in range(4):
        inner = dot(grad_inner[:, block * 512 : (block + 1) * 512], normed_mlp[...], 0, 0)
        outer = dot(cotangent[:, block * 128 : (block + 1) * 128], activated[...], 0, 0)
        terms = [inner.reshape(32, 16, WIDTH)]
        for part in range(4):
            terms.append(outer[:, part * WIDTH : (part + 1) * WIDTH].reshape(32, 4, WIDTH))
        put_terms(place, terms, block, pl.ds(16, 32), mine, others)


def row_terms(place, *refs):
    far, mine, others, near, semaphores = refs[:4], refs[4], refs[5:7], refs[7:11], refs[11]
    mover = Mover(semaphores)
    for copy in [mover.start(source, target) for source, target in zip(far, near)]:
        copy.wait()
    for block in range(4):
        terms = jnp.concatenate(block_terms(block, *near), axis=1)
        terms = terms.astype(bf16).reshape(16, 2, 16, WIDTH)
        mine[pl.ds(block * 16, 16)] = jnp.where(place[0] == 0, terms[:, 0], terms[:, 1])
        leaving = jnp.where(place[0] == 0, terms[:, 1], terms[:, 0])
        others[block // 2][pl.ds(block % 2 * 16, 16)] = leaving


def join_cores(mine, first, second, out):
    for block in range(4):
        chips = pl.ds(block * 16, 16)
        other = (first, second)[block // 2][pl.ds(block % 2 * 16, 16)]
        out[chips] = (mine[chips].astype(f32) + other.astype(f32)).astype(bf16)


def add_cores(mine, *refs):
    others, out_far, total, semaphores = refs[:5], *refs[5:]
    mover = Mover(semaphores)
    leaving = []
    for block in range(4):
        for place in range(16):
            row, rest = divmod(place, 4)
            high, low_z = divmod(rest, 2)
            piece, chip = divmod(16 * block + place, PIECE)
            own = mine[block, row, high, low_z].astype(f32)
            total[block, row, high, low_z] = (own + others[piece][chip].astype(f32)).astype(bf16)
        leaving.append(mover.start(total.at[block], out_far.at[block]))
    for copy in leaving:
        copy.wait()


def sum_row(parts, lon_in, lon_out):
    total = jnp.sum(parts[...].astype(f32), axis=0)
    lon_in[...] = total[0:12]
    lon_out[...] = total[12:16]


def pick_y(place, blocks_far, *refs):
    outs, mover = refs[:4], Mover(refs[4])
    copies = [
        mover.start(blocks_far.at[jnp.bitwise_xor(place[1], step)], outs[step]) for step in range(4)
    ]
    for copy in copies:
        copy.wait()


def sum_pick_z(place, *refs):
    parts, outs, total = refs[:4], refs[4:8], refs[8]
    added = sum(part[...].astype(f32) for part in parts)
    total[...] = added.astype(bf16).reshape(total.shape)
    for step in range(4):
        outs[step][...] = total[jnp.bitwise_xor(place[2], step)]


def sum_column(*refs):
    parts, (lat_in, lat_out, wide_in, wide_out) = refs[:4], refs[4:]
    total = sum(part[...].astype(f32) for part in parts)
    lat_in[...] = total[0:12]
    lat_out[...] = total[12:16]
    wide_in[...] = total[16:32]
    for part in range(4):
        wide_out[:, part * WIDTH : (part + 1) * WIDTH] = total[32 + 4 * part : 36 + 4 * part]


SMEM, VMEM, HBM = pltpu.SMEM, pltpu.VMEM, pltpu.HBM


def call(kernel, args, outs, scratch, semaphores, megabytes, gigaflops, aliases=None):
    arrays = [
        pltpu.with_memory_space_constraint(array, HBM) if place is HBM else array
        for array, place in args
    ]
    scratch = [pltpu.VMEM(shape, kind) for shape, kind in scratch]
    if semaphores:
        scratch.append(pltpu.SemaphoreType.DMA((semaphores,)))
    return pl.pallas_call(
        kernel,
        out_shape=[
            jax.ShapeDtypeStruct(shape, kind) if place is pl.ANY else place(shape, kind)
            for shape, kind, place in outs
        ],
        in_specs=[pl.BlockSpec(memory_space=place) for _, place in args],
        out_specs=[
            pl.BlockSpec(memory_space=VMEM if place is pl.ANY else place) for _, _, place in outs
        ],
        scratch_shapes=scratch,
        compiler_params=pltpu.CompilerParams(vmem_limit_bytes=megabytes << 20),
        cost_estimate=pl.CostEstimate(
            flops=int(gigaflops * 1e9), bytes_accessed=1 << 16, transcendentals=0
        ),
        input_output_aliases=aliases or {},
    )(*arrays)


def swap(array, axes):
    return lax.all_to_all(array, axes, split_axis=0, concat_axis=0, tiled=True)


def trade(parts, axes):
    moved = [
        lax.ppermute(parts[step], axes, [(place, place ^ step) for place in range(4)])
        for step in (2, 3, 1)
    ]
    return [parts[0], *moved]


def from_other_core(array):
    return lax.ppermute(array, "c", [(0, 1), (1, 0)])


NARROW = (ROWS, WIDTH)
QKV = (ROWS, 3 * WIDTH)
WIDE = (ROWS, FF)
TILES = (4, 2 * ROWS, 128)
TURNED = (WIDTH, ROWS)
TO_TURN = (LATS, 2 * PART, WIDTH)
TO_LON = (16, 2 * NEAR, WIDTH)
LON_WEIGHTS = (HEADS, ROWS, ROWS)
LAT_PROBS = (HEADS, LATS, ROWS)
IN, OUT, MLP_IN, MLP_OUT = (WIDTH, 3 * WIDTH), (WIDTH, WIDTH), (WIDTH, FF), (FF, WIDTH)
SUMS = (64, 16, WIDTH)
BY_CHIP = (4, 4, 2, 2, 48, WIDTH)


def low(*shapes):
    return [(shape, bf16) for shape in shapes]


def far(*shapes):
    return [(shape, bf16, HBM) for shape in shapes]


def all_far(*arrays):
    return [(array, HBM) for array in arrays]


def per_device(tokens, cotangent, inproj_lon, outproj_lon, inproj_lat, outproj_lat, mlp_in, mlp_out):
    core = jnp.stack([lax.axis_index(axes) for axes in ("c", "y", ("h", "l"))]).astype(jnp.int32)
    pack = jnp.concatenate([tokens, cotangent], axis=2).reshape(TO_LON)
    pack, row_tokens, row_normed, row_packed, row_mixed = call(
        row_forward,
        [(swap(pack, LON), VMEM)] + all_far(inproj_lon, outproj_lon),
        [(TO_TURN, bf16, VMEM)] + far(NARROW, NARROW, QKV, NARROW),
        low(IN, OUT, NARROW, NARROW, QKV, NARROW) + [(NARROW, f32), (NARROW, f32), (TURNED, f32)],
        6,
        20,
        5.0,
    )
    pack, normed, mixed, grads, upstream, *saved = call(
        column_both,
        [(swap(pack, TURN), VMEM)] + all_far(inproj_lat, outproj_lat, mlp_in, mlp_out),
        [(TO_TURN, bf16, VMEM)] + far(NARROW, NARROW, QKV, NARROW, NARROW, WIDE, WIDE, NARROW),
        low(IN, OUT, MLP_IN, MLP_OUT, NARROW, NARROW, QKV, NARROW, NARROW, WIDE, WIDE, NARROW, QKV, NARROW)
        + [(TILES, f32), (TURNED, f32)] + [(NARROW, f32)] * 4 + [(LAT_PROBS, f32)] * 2,
        12,
        36,
        20.0,
    )
    mine, *others = call(
        column_terms,
        [(core, SMEM)] + all_far(grads, normed, upstream, mixed, *(saved[i] for i in (0, 2, 1, 3))),
        [(BY_CHIP, bf16, VMEM)] + [((PIECE, 48, WIDTH), bf16, VMEM)] * 5,
        low(QKV, NARROW, NARROW, NARROW, NARROW, WIDE, WIDE, NARROW),
        8,
        32,
        0.1,
    )
    (weights,) = call(
        row_weights,
        [(row_packed, HBM), (mine, pl.ANY)],
        far(LON_WEIGHTS),
        low(QKV, LON_WEIGHTS),
        2,
        12,
        0.1,
    )
    (column,) = call(
        add_cores,
        [(mine, VMEM)] + [(from_other_core(other), VMEM) for other in others],
        far(BY_CHIP),
        low(BY_CHIP),
        4,
        20,
        0.1,
    )
    column = lax.psum_scatter(column.reshape(3072, WIDTH), "x", scatter_dimension=0, tiled=True)
    pack, grads, upstream = call(
        row_backward,
        [(swap(pack, TURN), VMEM)]
        + all_far(row_tokens, row_packed, weights, inproj_lon, outproj_lon),
        [(TO_LON, bf16, pl.ANY)] + far(QKV, NARROW),
        low(NARROW, QKV, LON_WEIGHTS, IN, OUT, QKV, NARROW)
        + [(NARROW, f32), (NARROW, f32), (NARROW, bf16)],
        7,
        28,
        60.0,
    )
    lon_mine, *lon_others = call(
        row_terms,
        [(core, SMEM)] + all_far(grads, row_normed, upstream, row_mixed),
        [(SUMS, bf16, VMEM)] + [((32, 16, WIDTH), bf16, VMEM)] * 2,
        low(QKV, NARROW, NARROW, NARROW),
        4,
        20,
        0.1,
    )
    pack = swap(pack, LON)
    (both,) = call(
        join_cores, [(lon_mine, VMEM)] + [(from_other_core(other), VMEM) for other in lon_others], [(SUMS, bf16, VMEM)], [], 0, 12, 0.1
    )
    unpacked = pack.reshape(4, 4, 2 * NEAR, WIDTH).astype(f32)
    lon = call(
        sum_row,
        [(swap(both, CHIPS), VMEM)],
        [((12, WIDTH), f32, pl.ANY), ((4, WIDTH), f32, pl.ANY)],
        [],
        0,
        12,
        60.0,
    )
    parts = call(
        pick_y,
        [(core, SMEM), (column.reshape(4, 192, WIDTH), HBM)],
        [((192, WIDTH), bf16, VMEM)] * 4,
        [],
        4,
        8,
        0.01,
    )
    parts = call(
        sum_pick_z,
        [(core, SMEM)] + [(part, VMEM) for part in trade(parts, "y")],
        [((48, WIDTH), bf16, VMEM)] * 4,
        low((4, 48, WIDTH)),
        0,
        8,
        0.01,
    )
    column = call(
        sum_column,
        [(part, VMEM) for part in trade(parts, ("h", "l"))],
        [((rows, lanes), f32, pl.ANY) for rows, lanes in ((12, WIDTH), (4, WIDTH), (16, WIDTH), (4, FF))],
        [],
        0,
        4,
        0.1,
    )
    return (
        unpacked[:, :, NEAR:],
        unpacked[:, :, :NEAR],
        *(array.T for array in lon),
        *(array.T for array in column),
    )


def solution(mesh):
    fine = Mesh(mesh.devices.reshape(4, 2, 4, 2, 2), ("x", "h", "y", "l", "c"))
    grid = P(("x", "h"), None, ("y", "l", "c"), None)
    columns = P(None, ("x", "h", "y", "l", "c"))
    return jax.shard_map(
        per_device,
        mesh=fine,
        in_specs=(grid, grid) + (P(),) * 6,
        out_specs=(grid, grid) + (columns,) * 6,
        check_vma=False,
    )
```

```python
import jax
import jax.numpy as jnp
from jax import lax
from jax.experimental import pallas as pl
from jax.experimental.pallas import tpu as pltpu
from jax.sharding import Mesh, PartitionSpec as P

HEADS = 8
WIDTH = 512
FF = 2048
HEAD = WIDTH // HEADS
SCALE = HEAD**-0.5
EPSILON = 1e-05
ROWS = 352
LATS = 32
NEAR = 22
PART = 11
PIECE = 13
LON = ("y", "l", "c")
TURN = ("h", "x", "y")
CHIPS = ("x", "h", "y", "l")
UNROLL = HEADS // 2
BLOCKS = ((0, 128), (128, 128), (256, 96))
f32 = jnp.float32
bf16 = jnp.bfloat16


def normalize(values):
    center = values - jnp.mean(values, axis=-1, keepdims=True)
    inverse = lax.rsqrt(jnp.mean(center * center, axis=-1, keepdims=True) + EPSILON)
    return center * inverse, inverse


def norm_back(scaled, inverse, upstream):
    return inverse * (
        upstream
        - jnp.mean(upstream, axis=-1, keepdims=True)
        - scaled * jnp.mean(upstream * scaled, axis=-1, keepdims=True)
    )


def dot(left, right, left_dim=1, right_dim=0):
    dims = (((left_dim,), (right_dim,)), ((), ()))
    return lax.dot_general(left, right, dims, preferred_element_type=f32)


def half_of(values, half):
    lanes = lax.broadcasted_iota(jnp.int32, values.shape, 1) // HEAD
    return jnp.where(lanes == half, values, jnp.zeros_like(values))


def pair_columns(part, pair):
    return pl.ds(pl.multiple_of(part * WIDTH + pair * 2 * HEAD, 2 * HEAD), 2 * HEAD)


def over_pairs(body):
    lax.fori_loop(0, HEADS // 2, lambda pair, _: body(pair) or 0, 0, unroll=UNROLL)


def row_probabilities(packed, pair, half):
    keys = half_of(packed[:, pair_columns(1, pair)] * SCALE, half)
    scores = dot(keys, packed[:, pair_columns(0, pair)], 1, 1)
    powers = jnp.exp(scores - jnp.max(scores, axis=0, keepdims=True))
    return (powers * (1.0 / jnp.sum(powers, axis=0, keepdims=True))).astype(bf16)


def put_mixed(turned, pair, half, rows, mixed):
    place = pl.ds(pl.multiple_of(pair * 2 * HEAD + half * HEAD, HEAD), HEAD)
    turned[place, rows] = mixed[half * HEAD : (half + 1) * HEAD]


def put_grads(grads, pair, rows, found):
    for part in range(3):
        both = half_of(found[0][part], 0) + half_of(found[1][part], 1)
        grads[rows, pair_columns(part, pair)] = both.astype(bf16)


def attend_rows(packed, turned):
    def one_pair(pair):
        values = packed[:, pair_columns(2, pair)]
        probs = [row_probabilities(packed, pair, half) for half in range(2)]
        for half in range(2):
            put_mixed(turned, pair, half, pl.ds(0, ROWS), dot(values, probs[half], 0, 0))

    over_pairs(one_pair)


def row_weights(packed_far, after, weights_far, packed, weights, semaphores):
    mover = Mover(semaphores)
    del after
    mover.start(packed_far, packed).wait()

    def one_pair(pair):
        for half in range(2):
            weights[pair * 2 + half] = row_probabilities(packed, pair, half)

    over_pairs(one_pair)
    mover.start(weights, weights_far).wait()


def attend_rows_back(packed, upstream, weights, grads):
    def one_pair(pair):
        queries, keys, values = (packed[:, pair_columns(p, pair)] for p in range(3))
        grad_mix = upstream[:, pair_columns(0, pair)]
        found = []
        for half in range(2):
            low = weights[pair * 2 + half]
            probs = low.astype(f32)
            grad_probs = dot(half_of(values, half), grad_mix, 1, 1)
            inner = jnp.sum(grad_probs * probs, axis=0, keepdims=True)
            grad_scores = (probs * (grad_probs - inner) * SCALE).astype(bf16)
            found.append(
                (dot(grad_scores, keys, 0, 0), dot(grad_scores, queries), dot(low, grad_mix))
            )
        put_grads(grads, pair, pl.ds(0, ROWS), found)

    over_pairs(one_pair)


def column_lanes(count):
    return lax.broadcasted_iota(jnp.int32, (LATS, count), 1) // LATS


def own_columns(square):
    count = square.shape[0]
    lanes = column_lanes(count)
    kept = square[:LATS]
    for column in range(1, count // LATS):
        kept = jnp.where(lanes == column, square[column * LATS : (column + 1) * LATS], kept)
    return kept


def to_square(kept):
    count = kept.shape[1]
    lanes = column_lanes(count)
    parts = [jnp.where(lanes == column, kept, 0.0) for column in range(count // LATS)]
    return jnp.concatenate(parts, axis=0).astype(bf16)


def attend_columns(packed, turned, probs):
    def scores(pair):
        for first, count in BLOCKS:
            rows = pl.ds(first, count)
            queries, keys = (packed[rows, pair_columns(p, pair)] for p in range(2))
            for half in range(2):
                square = dot(half_of(keys * SCALE, half), queries, 1, 1)
                probs[pair * 2 + half, :, rows] = own_columns(square)

    over_pairs(scores)
    powers = probs[...]
    powers = jnp.exp(powers - jnp.max(powers, axis=1, keepdims=True))
    probs[...] = powers * (1.0 / jnp.sum(powers, axis=1, keepdims=True))

    def mix(pair):
        for first, count in BLOCKS:
            rows = pl.ds(first, count)
            values = packed[rows, pair_columns(2, pair)]
            for half in range(2):
                square = to_square(probs[pair * 2 + half, :, rows])
                put_mixed(turned, pair, half, rows, dot(values, square, 0, 0))

    over_pairs(mix)


def attend_columns_back(packed, upstream, probs, grad_scores, grads):
    def products(pair):
        for first, count in BLOCKS:
            rows = pl.ds(first, count)
            values, grad_mix = packed[rows, pair_columns(2, pair)], upstream[rows, pair_columns(0, pair)]
            for half in range(2):
                square = dot(half_of(values, half), grad_mix, 1, 1)
                grad_scores[pair * 2 + half, :, rows] = own_columns(square)

    over_pairs(products)
    grad_probs = grad_scores[...]
    inner = jnp.sum(grad_probs * probs[...], axis=1, keepdims=True)
    grad_scores[...] = probs[...] * (grad_probs - inner) * SCALE

    def combine(pair):
        for first, count in BLOCKS:
            rows = pl.ds(first, count)
            queries, keys = (packed[rows, pair_columns(p, pair)] for p in range(2))
            grad_mix = upstream[rows, pair_columns(0, pair)]
            found = []
            for half in range(2):
                square = to_square(grad_scores[pair * 2 + half, :, rows])
                weights = to_square(probs[pair * 2 + half, :, rows])
                found.append(
                    (dot(square, keys, 0, 0), dot(square, queries), dot(weights, grad_mix))
                )
            put_grads(grads, pair, rows, found)

    over_pairs(combine)


def project(normed, inproj, packed):
    for part in range(3):
        columns = pl.ds(part * WIDTH, WIDTH)
        packed[:, columns] = dot(normed, inproj[:, columns]).astype(bf16)


class Mover:
    def __init__(self, semaphores):
        self.semaphores, self.count = semaphores, 0

    def start(self, source, target):
        copy = pltpu.make_async_copy(source, target, self.semaphores.at[self.count])
        self.count += 1
        copy.start()
        return copy


def row_forward(
    pack, inproj_far, outproj_far,
    out, tokens_far, normed_far, packed_far, mixed_far,
    inproj, outproj, tokens, normed, packed, mixed, hidden, cotangent, turned, semaphores,
):
    mover = Mover(semaphores)
    inproj_in = mover.start(inproj_far, inproj)
    outproj_in = mover.start(outproj_far, outproj)
    for block in range(16):
        piece = pack[block].astype(f32)
        rows = pl.ds(block * NEAR, NEAR)
        hidden[rows, :] = piece[:NEAR]
        cotangent[rows, :] = piece[NEAR:]
    values = hidden[:ROWS]
    tokens[...] = values.astype(bf16)
    normed[...] = normalize(values)[0].astype(bf16)
    leaving = [mover.start(tokens, tokens_far), mover.start(normed, normed_far)]
    inproj_in.wait()
    project(normed[...], inproj, packed)
    leaving.append(mover.start(packed, packed_far))
    attend_rows(packed, turned)
    mixed[...] = turned[...].T.astype(bf16)
    leaving.append(mover.start(mixed, mixed_far))
    outproj_in.wait()
    hidden[:ROWS] += dot(mixed[...], outproj[...])
    for block in range(LATS):
        rows = pl.ds(block * PART, PART)
        out[block] = jnp.concatenate([hidden[rows, :], cotangent[rows, :]], axis=0).astype(bf16)
    for copy in leaving:
        copy.wait()


def row_backward(
    pack, tokens_far, packed_far, weights_far, inproj_far, outproj_far,
    out, grads_far, low_far,
    tokens, packed, weights, inproj, outproj, grads, low, hidden, output, upstream, semaphores,
):
    mover = Mover(semaphores)
    outproj_in = mover.start(outproj_far, outproj)
    coming = [mover.start(packed_far, packed), mover.start(weights_far, weights)]
    inproj_in = mover.start(inproj_far, inproj)
    tokens_in = mover.start(tokens_far, tokens)
    for block in range(LATS):
        piece = pack[block].astype(f32)
        rows = pl.ds(block * PART, PART)
        hidden[rows, :] = piece[:PART]
        output[rows, :] = piece[PART:]
    low[...] = hidden[:ROWS].astype(bf16)
    leaving = [mover.start(low, low_far)]
    outproj_in.wait()
    upstream[...] = dot(low[...], outproj[...], 1, 1).astype(bf16)
    for copy in coming:
        copy.wait()
    attend_rows_back(packed, upstream, weights, grads)
    leaving.append(mover.start(grads, grads_far))
    inproj_in.wait()
    grad_normed = dot(grads[...], inproj[...], 1, 1)
    tokens_in.wait()
    hidden[:ROWS] += norm_back(*normalize(tokens[...].astype(f32)), grad_normed)
    for block in range(16):
        rows = pl.ds(block * NEAR, NEAR)
        out[block] = jnp.concatenate([hidden[rows, :], output[rows, :]], axis=0).astype(bf16)
    for copy in leaving:
        copy.wait()


def to_columns(pack, columns):
    for lat in range(LATS):
        piece = pack[lat].astype(f32)
        for tile in range(4):
            lanes = slice(tile * 128, (tile + 1) * 128)
            columns[tile, pl.ds(lat, 2 * PART, stride=LATS), :] = piece[:, lanes]


def joined(columns, unit):
    rows = pl.ds(unit * ROWS, ROWS)
    return jnp.concatenate([columns[tile, rows, :] for tile in range(4)], axis=1)


def put_columns(columns, unit, values):
    for tile in range(4):
        columns[tile, pl.ds(unit * ROWS, ROWS), :] = values[:, tile * 128 : (tile + 1) * 128]


def from_columns(out, columns):
    for lat in range(LATS):
        rows = pl.ds(lat, 2 * PART, stride=LATS)
        piece = jnp.concatenate([columns[tile, rows, :] for tile in range(4)], axis=1)
        out[lat] = piece.astype(bf16)


def column_both(
    pack, inproj_far, outproj_far, mlp_in_far, mlp_out_far,
    out, normed_far, mixed_far, grads_far, low_far, normed_mlp_far, activated_far, grad_inner_far, cotangent_far,
    inproj, outproj, mlp_in, mlp_out, normed, mixed, grads, low, normed_mlp, activated, grad_inner, cotangent,
    packed, upstream, columns, turned, hidden_one, hidden, grad_normed, output, probs, grad_scores,
    semaphores,
):
    mover = Mover(semaphores)
    inproj_in = mover.start(inproj_far, inproj)
    outproj_in = mover.start(outproj_far, outproj)
    coming = [mover.start(mlp_in_far, mlp_in), mover.start(mlp_out_far, mlp_out)]
    to_columns(pack, columns)
    hidden_one[...] = joined(columns, 0)
    cotangent[...] = joined(columns, 1).astype(bf16)
    normed[...] = normalize(hidden_one[...])[0].astype(bf16)
    leaving = [mover.start(cotangent, cotangent_far), mover.start(normed, normed_far)]
    inproj_in.wait()
    project(normed[...], inproj, packed)
    attend_columns(packed, turned, probs)
    mixed[...] = turned[...].T.astype(bf16)
    leaving.append(mover.start(mixed, mixed_far))
    outproj_in.wait()
    hidden[...] = hidden_one[...] + dot(mixed[...], outproj[...])
    normed_mlp[...] = normalize(hidden[...])[0].astype(bf16)
    leaving.append(mover.start(normed_mlp, normed_mlp_far))
    output[...] = hidden[...]
    grad_normed[...] = jnp.zeros_like(grad_normed)
    for copy in coming:
        copy.wait()

    def one_chunk(chunk, _):
        chosen = pl.ds(pl.multiple_of(chunk * 512, 512), 512)
        inner = dot(normed_mlp[...], mlp_in[:, chosen])
        spread = 0.5 * (1.0 + lax.erf(inner * 2.0**-0.5))
        slope = spread + inner * (0.5 / jnp.pi) ** 0.5 * jnp.exp(-0.5 * inner * inner)
        active = (inner * spread).astype(bf16)
        activated[:, chosen] = active
        output[...] += dot(active, mlp_out[chosen, :])
        grad = (dot(cotangent[...], mlp_out[chosen, :], 1, 1) * slope).astype(bf16)
        grad_inner[:, chosen] = grad
        grad_normed[...] += dot(grad, mlp_in[:, chosen], 1, 1)
        return 0

    lax.fori_loop(0, FF // 512, one_chunk, 0, unroll=4)
    leaving.append(mover.start(activated, activated_far))
    leaving.append(mover.start(grad_inner, grad_inner_far))
    put_columns(columns, 1, output[...])
    back = norm_back(*normalize(hidden[...]), grad_normed[...])
    hidden[...] = cotangent[...].astype(f32) + back
    low[...] = hidden[...].astype(bf16)
    leaving.append(mover.start(low, low_far))
    upstream[...] = dot(low[...], outproj[...], 1, 1).astype(bf16)
    attend_columns_back(packed, upstream, probs, grad_scores, grads)
    leaving.append(mover.start(grads, grads_far))
    back = norm_back(*normalize(hidden_one[...]), dot(grads[...], inproj[...], 1, 1))
    put_columns(columns, 0, hidden[...] + back)
    from_columns(out, columns)
    for copy in leaving:
        copy.wait()


def block_terms(block, grads, normed, low, mixed):
    wide = dot(grads[:, block * 384 : (block + 1) * 384], normed[...], 0, 0)
    slim = dot(low[:, block * 128 : (block + 1) * 128], mixed[...], 0, 0)
    return [wide.reshape(32, 12, WIDTH), slim.reshape(32, 4, WIDTH)]


def put_terms(place, terms, block, rows, mine, others):
    both = jnp.concatenate(terms, axis=1).astype(bf16)
    both = both.reshape(2, 4, 2, 2, both.shape[1], WIDTH)
    for high in range(2):
        even, odd = both[high, :, :, 0], both[high, :, :, 1]
        mine[block, :, high, :, rows, :] = jnp.where(place[0] == 0, even, odd)
        leaving = jnp.where(place[0] == 0, odd, even)
        for row in range(4):
            for low_z in range(2):
                piece, chip = divmod(16 * block + 4 * row + 2 * high + low_z, PIECE)
                others[piece][chip, rows, :] = leaving[row, low_z]


def column_terms(place, *refs):
    far, mine, others, near, semaphores = refs[:8], refs[8], refs[9:14], refs[14:22], refs[22]
    mover = Mover(semaphores)
    coming = [mover.start(source, target) for source, target in zip(far, near)]
    grads, normed, low, mixed, normed_mlp, grad_inner, activated, cotangent = near
    for copy in coming[:4]:
        copy.wait()
    for block in range(4):
        terms = block_terms(block, grads, normed, low, mixed)
        put_terms(place, terms, block, pl.ds(0, 16), mine, others)
    for copy in coming[4:]:
        copy.wait()
    for block in range(4):
        inner = dot(grad_inner[:, block * 512 : (block + 1) * 512], normed_mlp[...], 0, 0)
        outer = dot(cotangent[:, block * 128 : (block + 1) * 128], activated[...], 0, 0)
        terms = [inner.reshape(32, 16, WIDTH)]
        for part in range(4):
            terms.append(outer[:, part * WIDTH : (part + 1) * WIDTH].reshape(32, 4, WIDTH))
        put_terms(place, terms, block, pl.ds(16, 32), mine, others)


def row_terms(place, *refs):
    far, mine, others, near, semaphores = refs[:4], refs[4], refs[5:7], refs[7:11], refs[11]
    mover = Mover(semaphores)
    for copy in [mover.start(source, target) for source, target in zip(far, near)]:
        copy.wait()
    for block in range(4):
        terms = jnp.concatenate(block_terms(block, *near), axis=1)
        terms = terms.astype(bf16).reshape(16, 2, 16, WIDTH)
        mine[pl.ds(block * 16, 16)] = jnp.where(place[0] == 0, terms[:, 0], terms[:, 1])
        leaving = jnp.where(place[0] == 0, terms[:, 1], terms[:, 0])
        others[block // 2][pl.ds(block % 2 * 16, 16)] = leaving


def join_cores(mine, first, second, out):
    for block in range(4):
        chips = pl.ds(block * 16, 16)
        other = (first, second)[block // 2][pl.ds(block % 2 * 16, 16)]
        out[chips] = (mine[chips].astype(f32) + other.astype(f32)).astype(bf16)


def add_cores(mine, *refs):
    others, out_far, total, semaphores = refs[:5], *refs[5:]
    mover = Mover(semaphores)
    leaving = []
    for block in range(4):
        for place in range(16):
            row, rest = divmod(place, 4)
            high, low_z = divmod(rest, 2)
            piece, chip = divmod(16 * block + place, PIECE)
            own = mine[block, row, high, low_z].astype(f32)
            total[block, row, high, low_z] = (own + others[piece][chip].astype(f32)).astype(bf16)
        leaving.append(mover.start(total.at[block], out_far.at[block]))
    for copy in leaving:
        copy.wait()


def sum_row(parts, lon_in, lon_out):
    total = jnp.sum(parts[...].astype(f32), axis=0)
    lon_in[...] = total[0:12]
    lon_out[...] = total[12:16]


def pick_y(place, blocks_far, *refs):
    outs, mover = refs[:4], Mover(refs[4])
    copies = [
        mover.start(blocks_far.at[jnp.bitwise_xor(place[1], step)], outs[step]) for step in range(4)
    ]
    for copy in copies:
        copy.wait()


def sum_pick_z(place, *refs):
    parts, outs, total = refs[:4], refs[4:8], refs[8]
    added = sum(part[...].astype(f32) for part in parts)
    total[...] = added.astype(bf16).reshape(total.shape)
    for step in range(4):
        outs[step][...] = total[jnp.bitwise_xor(place[2], step)]


def sum_column(*refs):
    parts, (lat_in, lat_out, wide_in, wide_out) = refs[:4], refs[4:]
    total = sum(part[...].astype(f32) for part in parts)
    lat_in[...] = total[0:12]
    lat_out[...] = total[12:16]
    wide_in[...] = total[16:32]
    for part in range(4):
        wide_out[:, part * WIDTH : (part + 1) * WIDTH] = total[32 + 4 * part : 36 + 4 * part]


SMEM, VMEM, HBM = pltpu.SMEM, pltpu.VMEM, pltpu.HBM


def call(kernel, args, outs, scratch, semaphores, megabytes, gigaflops, aliases=None):
    arrays = [
        pltpu.with_memory_space_constraint(array, HBM) if place is HBM else array
        for array, place in args
    ]
    scratch = [pltpu.VMEM(shape, kind) for shape, kind in scratch]
    if semaphores:
        scratch.append(pltpu.SemaphoreType.DMA((semaphores,)))
    return pl.pallas_call(
        kernel,
        out_shape=[
            jax.ShapeDtypeStruct(shape, kind) if place is pl.ANY else place(shape, kind)
            for shape, kind, place in outs
        ],
        in_specs=[pl.BlockSpec(memory_space=place) for _, place in args],
        out_specs=[
            pl.BlockSpec(memory_space=VMEM if place is pl.ANY else place) for _, _, place in outs
        ],
        scratch_shapes=scratch,
        compiler_params=pltpu.CompilerParams(vmem_limit_bytes=megabytes << 20),
        cost_estimate=pl.CostEstimate(
            flops=int(gigaflops * 1e9), bytes_accessed=1 << 16, transcendentals=0
        ),
        input_output_aliases=aliases or {},
    )(*arrays)


def swap(array, axes):
    return lax.all_to_all(array, axes, split_axis=0, concat_axis=0, tiled=True)


def trade(parts, axes):
    moved = [
        lax.ppermute(parts[step], axes, [(place, place ^ step) for place in range(4)])
        for step in (2, 3, 1)
    ]
    return [parts[0], *moved]


def from_other_core(array):
    return lax.ppermute(array, "c", [(0, 1), (1, 0)])


NARROW = (ROWS, WIDTH)
QKV = (ROWS, 3 * WIDTH)
WIDE = (ROWS, FF)
TILES = (4, 24 * LATS, 128)
ROOMY = (ROWS + 8, WIDTH)
TURNED = (WIDTH, ROWS)
TO_TURN = (LATS, 2 * PART, WIDTH)
TO_LON = (16, 2 * NEAR, WIDTH)
LON_WEIGHTS = (HEADS, ROWS, ROWS)
LAT_PROBS = (HEADS, LATS, ROWS)
IN, OUT, MLP_IN, MLP_OUT = (WIDTH, 3 * WIDTH), (WIDTH, WIDTH), (WIDTH, FF), (FF, WIDTH)
SUMS = (64, 16, WIDTH)
BY_CHIP = (4, 4, 2, 2, 48, WIDTH)


def low(*shapes):
    return [(shape, bf16) for shape in shapes]


def far(*shapes):
    return [(shape, bf16, HBM) for shape in shapes]


def all_far(*arrays):
    return [(array, HBM) for array in arrays]


def per_device(tokens, cotangent, inproj_lon, outproj_lon, inproj_lat, outproj_lat, mlp_in, mlp_out):
    core = jnp.stack([lax.axis_index(axes) for axes in ("c", "y", ("h", "l"))]).astype(jnp.int32)
    pack = jnp.concatenate([tokens, cotangent], axis=2).reshape(TO_LON)
    pack, row_tokens, row_normed, row_packed, row_mixed = call(
        row_forward,
        [(swap(pack, LON), VMEM)] + all_far(inproj_lon, outproj_lon),
        [(TO_TURN, bf16, VMEM)] + far(NARROW, NARROW, QKV, NARROW),
        low(IN, OUT, NARROW, NARROW, QKV, NARROW) + [(ROOMY, f32), (ROOMY, f32), (TURNED, f32)],
        6,
        20,
        5.0,
    )
    pack, normed, mixed, grads, upstream, *saved = call(
        column_both,
        [(swap(pack, TURN), VMEM)] + all_far(inproj_lat, outproj_lat, mlp_in, mlp_out),
        [(TO_TURN, bf16, VMEM)] + far(NARROW, NARROW, QKV, NARROW, NARROW, WIDE, WIDE, NARROW),
        low(IN, OUT, MLP_IN, MLP_OUT, NARROW, NARROW, QKV, NARROW, NARROW, WIDE, WIDE, NARROW, QKV, NARROW)
        + [(TILES, f32), (TURNED, f32)] + [(NARROW, f32)] * 4 + [(LAT_PROBS, f32)] * 2,
        12,
        36,
        20.0,
    )
    mine, *others = call(
        column_terms,
        [(core, SMEM)] + all_far(grads, normed, upstream, mixed, *(saved[i] for i in (0, 2, 1, 3))),
        [(BY_CHIP, bf16, VMEM)] + [((PIECE, 48, WIDTH), bf16, VMEM)] * 5,
        low(QKV, NARROW, NARROW, NARROW, NARROW, WIDE, WIDE, NARROW),
        8,
        32,
        0.1,
    )
    (weights,) = call(
        row_weights,
        [(row_packed, HBM), (mine, pl.ANY)],
        far(LON_WEIGHTS),
        low(QKV, LON_WEIGHTS),
        2,
        12,
        0.1,
    )
    (column,) = call(
        add_cores,
        [(mine, VMEM)] + [(from_other_core(other), VMEM) for other in others],
        far(BY_CHIP),
        low(BY_CHIP),
        4,
        20,
        0.1,
    )
    column = lax.psum_scatter(column.reshape(3072, WIDTH), "x", scatter_dimension=0, tiled=True)
    pack, grads, upstream = call(
        row_backward,
        [(swap(pack, TURN), VMEM)]
        + all_far(row_tokens, row_packed, weights, inproj_lon, outproj_lon),
        [(TO_LON, bf16, pl.ANY)] + far(QKV, NARROW),
        low(NARROW, QKV, LON_WEIGHTS, IN, OUT, QKV, NARROW)
        + [(ROOMY, f32), (ROOMY, f32), (NARROW, bf16)],
        7,
        28,
        60.0,
    )
    lon_mine, *lon_others = call(
        row_terms,
        [(core, SMEM)] + all_far(grads, row_normed, upstream, row_mixed),
        [(SUMS, bf16, VMEM)] + [((32, 16, WIDTH), bf16, VMEM)] * 2,
        low(QKV, NARROW, NARROW, NARROW),
        4,
        20,
        0.1,
    )
    pack = swap(pack, LON)
    (both,) = call(
        join_cores, [(lon_mine, VMEM)] + [(from_other_core(other), VMEM) for other in lon_others], [(SUMS, bf16, VMEM)], [], 0, 12, 0.1
    )
    unpacked = pack.reshape(4, 4, 2 * NEAR, WIDTH).astype(f32)
    lon = call(
        sum_row,
        [(swap(both, CHIPS), VMEM)],
        [((12, WIDTH), f32, pl.ANY), ((4, WIDTH), f32, pl.ANY)],
        [],
        0,
        12,
        60.0,
    )
    parts = call(
        pick_y,
        [(core, SMEM), (column.reshape(4, 192, WIDTH), HBM)],
        [((192, WIDTH), bf16, VMEM)] * 4,
        [],
        4,
        8,
        0.01,
    )
    parts = call(
        sum_pick_z,
        [(core, SMEM)] + [(part, VMEM) for part in trade(parts, "y")],
        [((48, WIDTH), bf16, VMEM)] * 4,
        low((4, 48, WIDTH)),
        0,
        8,
        0.01,
    )
    column = call(
        sum_column,
        [(part, VMEM) for part in trade(parts, ("h", "l"))],
        [((rows, lanes), f32, pl.ANY) for rows, lanes in ((12, WIDTH), (4, WIDTH), (16, WIDTH), (4, FF))],
        [],
        0,
        4,
        0.1,
    )
    return (
        unpacked[:, :, NEAR:],
        unpacked[:, :, :NEAR],
        *(array.T for array in lon),
        *(array.T for array in column),
    )


def solution(mesh):
    fine = Mesh(mesh.devices.reshape(4, 2, 4, 2, 2), ("x", "h", "y", "l", "c"))
    grid = P(("x", "h"), None, ("y", "l", "c"), None)
    columns = P(None, ("x", "h", "y", "l", "c"))
    return jax.shard_map(
        per_device,
        mesh=fine,
        in_specs=(grid, grid) + (P(),) * 6,
        out_specs=(grid, grid) + (columns,) * 6,
        check_vma=False,
    )
```
